1024 devices in a mesh: dom: 128 (over x, z, core), cls: 8 (over y).
Axes of the slice: x: 8, y: 8, z: 8, core: 2. Of those that a mesh axis runs over, the one named last changes fastest.
Arguments:
- tiles: bfloat16 [4096, 128, 128], P('dom'), may hold values from 0.0009994507 to 1
- tile_rows: int32 [4096], P('dom'), may hold values from 0 to 7
- tile_cols: int32 [4096], P('dom'), may hold values from 0 to 15
- send_lists: int32 [128, 4, 2], P('dom'), may hold values from 0 to 7
- seed_mask: int32 [131072], P('dom'), may hold values 0 or 1
- labels: float32 [131072, 1024], P('dom', 'cls'), may hold values from 0.1 to 10
Outputs:
- relabeled: float32 [131072, 1024], P('dom', 'cls')
The draws below stay inside these ranges and needn't reach their ends.
All inputs are finite; a program needn't handle non-finite values. No bound on the sum of `seed_mask` on one device may be relied on, other than what follows from the above.
Results may differ from the reference program's by a relative error of at most 0.0003.
Values sent between devices are 32-bit elements; how exact they have to be, the bound alone decides.
No kernel may reach another device: no remote copies, remote signals or barrier semaphores. Data moves between devices by JAX's collectives and lax.ppermute only.
A program may use at most 32 MiB of HBM per device.

```python
import math
import jax
import jax.numpy as jnp
from jax import lax

CLASSES = 1024
BLK = 128
BLK_DEV = 8
GHOSTS = 2
ITERS = 3
TILE_DEV = 32
PARTITIONS = 128
VERTICES = 131072
TILES = 4096


def set_ends(result, rng, least, top_value):
    longest = result.shape.index(max(result.shape))
    spots = []
    for shift in (0, 1):
        where = [jax.random.randint(jax.random.fold_in(rng, axis), (), 0, length) for axis, length in enumerate(result.shape)]
        where[longest] = (where[longest] + shift) % result.shape[longest]
        spots.append(tuple(where))
    return result.at[spots[0]].set(least).at[spots[1]].set(top_value)


def steps_of(stream_key, shape, pieces, least, high):
    def one(axis_at, blocks):
        steps = jax.random.uniform(jax.random.fold_in(jax.random.fold_in(stream_key, 6), axis_at), (blocks,), jnp.float32, least / len(pieces), high / len(pieces))
        return jnp.repeat(jnp.exp(steps), shape[axis_at] // blocks).reshape((-1,) + (1,) * (len(shape) - axis_at - 1))

    gain = one(*pieces[0])
    for cut in pieces[1:]:
        gain = gain * one(*cut)
    return gain


def setup_inputs(seed: int = 0) -> dict:
    splits = jax.random.split(jax.random.key(seed), 7)
    return {
        "tiles": jnp.clip(jnp.exp(math.log(1.0) - 6.9083047 * jax.random.uniform(splits[0], (TILES, BLK, BLK), jnp.float32) ** steps_of(splits[0], (TILES, BLK, BLK), ((0, 128),), -0.2, 0.2)), 0.0009994507, 1.0).astype(jnp.bfloat16),
        "tile_rows": set_ends(jax.random.randint(splits[1], (TILES,), 0, BLK_DEV), jax.random.fold_in(splits[1], 1), 0, BLK_DEV - 1).astype(jnp.int32),
        "tile_cols": set_ends(jax.random.randint(splits[2], (TILES,), 0, BLK_DEV + 4 * GHOSTS), jax.random.fold_in(splits[2], 1), 0, (BLK_DEV + 4 * GHOSTS) - 1).astype(jnp.int32),
        "send_lists": set_ends(jax.random.randint(splits[3], (PARTITIONS, 4, GHOSTS), 0, BLK_DEV), jax.random.fold_in(splits[3], 1), 0, BLK_DEV - 1).astype(jnp.int32),
        "seed_mask": set_ends((jax.random.randint(splits[4], (VERTICES,), 0, 4) < 1).astype(jnp.int32), jax.random.fold_in(splits[4], 1), 0, 1),
        "labels": jnp.clip(jnp.exp(math.log(10.0) - 4.6051702 * jax.random.uniform(splits[5], (VERTICES, CLASSES), jnp.float32) ** steps_of(splits[5], (VERTICES, CLASSES), ((0, 128), (1, 8)), -0.2, 0.2)), 0.1, 10.0),
    }


offsets_table = (1, 2, -1, -2)


def block_indices(tile_rows, tile_cols, send_lists):
    tile_count = tile_cols.shape[0]
    owner = (jnp.arange(tile_count, dtype=jnp.int32) // TILE_DEV).astype(jnp.int32)
    is_local = tile_cols < BLK_DEV
    ghost_slot = jnp.maximum(tile_cols - BLK_DEV, 0).astype(jnp.int32)
    position = (ghost_slot // GHOSTS).astype(jnp.int32)
    within = (ghost_slot % GHOSTS).astype(jnp.int32)
    offsets = jnp.array(offsets_table, dtype=jnp.int32)[position]
    sender = ((owner - offsets) % PARTITIONS).astype(jnp.int32)
    remote = sender * BLK_DEV + send_lists[sender, position, within]
    columns = jnp.where(is_local, owner * BLK_DEV + tile_cols, remote).astype(jnp.int32)
    row_blocks = (owner * BLK_DEV + tile_rows).astype(jnp.int32)
    return row_blocks, columns


def reference(tiles, tile_rows, tile_cols, send_lists, seed_mask, labels):
    block_count = labels.shape[0] // BLK
    blocks = labels.reshape(block_count, BLK, CLASSES)
    first_mass = jnp.sum(blocks, axis=2, keepdims=True)
    seeded_prior = CLASSES * blocks / first_mass
    seeded = seed_mask.reshape(block_count, BLK, 1).astype(jnp.float32)
    anchor = 64.0 * seeded * seeded_prior + 4.0
    row_blocks, columns = block_indices(tile_rows, tile_cols, send_lists)
    current = seeded_prior
    for iteration in range(ITERS):
        def add_tile(index, total):
            column = lax.dynamic_index_in_dim(current, columns[index], 0, keepdims=False)
            weights = lax.dynamic_index_in_dim(tiles, index, 0, keepdims=False).astype(jnp.float32)
            term = jnp.dot(weights, column, precision=lax.Precision.HIGHEST, preferred_element_type=jnp.float32)
            return total.at[row_blocks[index]].add(term)
        spread = lax.fori_loop(0, tiles.shape[0], add_tile, jnp.zeros(current.shape, jnp.float32))
        mixture = spread + anchor
        squared = mixture * mixture
        row_mass = jnp.sum(squared, axis=2, keepdims=True)
        current = CLASSES * squared / row_mass
    return current.reshape(block_count * BLK, CLASSES)
```

```python
import jax
import jax.numpy as jnp
from jax import lax
from jax.experimental import pallas as pl
from jax.experimental.pallas import tpu as pltpu
from jax.sharding import PartitionSpec as P

CLASSES = 1024
ITERS = 3
SIDE = 128

VMEM = pl.BlockSpec(memory_space=pltpu.VMEM)
SMEM = pl.BlockSpec(memory_space=pltpu.SMEM)
F32 = jnp.float32
PARAMS = pltpu.CompilerParams(vmem_limit_bytes=16 * 1024 * 1024)


def shape(*dims):
    return jax.ShapeDtypeStruct(dims, F32)


def send_slot(position, odd):
    if position == 0:
        return 2 * odd
    if position == 1:
        return 2 - 2 * odd
    return 1 if position == 2 else 3


def buffer_block(col, odd):
    ghost = jnp.maximum(col - 8, 0)
    offset = lax.shift_right_logical(ghost, 1)
    near = jnp.where(offset == 0, 1 - odd, odd)
    pair = jnp.where(lax.rem(offset, 2) == 1, 2 + lax.shift_right_logical(offset, 1), near)
    return jnp.where(col < 8, col, 8 + 2 * pair + lax.rem(ghost, 2))


def parity():
    return lax.rem(lax.axis_index("dom"), 2)


def gather(source, send, outgoing):
    odd = parity()
    for position in range(4):
        slot = send_slot(position, odd)
        for within in range(2):
            outgoing[position][within] = source[send[0, slot, within]]


def lane_sums(block):
    return jnp.sum(jnp.transpose(block), axis=0, keepdims=True)


def first_kernel(labels, send, out0, out1, out2, out3, own):
    gather(labels, send, (out0, out1, out2, out3))
    for block in range(8):
        own[block : block + 1, :] = lane_sums(labels[block])


def mass_kernel(own, in0, in1, in2, in3, parts):
    rows = [own[...]]
    for pair in (in0, in1, in2, in3):
        for within in range(2):
            rows.append(lane_sums(pair[within]))
    partial = jnp.concatenate(rows, axis=0)
    for share in range(8):
        parts[share] = partial


def scales(parts, blocks):
    total = parts[0]
    for share in range(1, 8):
        total = total + parts[share]
    scale = CLASSES / total
    full = jnp.concatenate([scale, jnp.zeros((SIDE - blocks, SIDE), F32)], axis=0)
    return jnp.transpose(full)


def split(value):
    high = value.astype(jnp.bfloat16)
    low = (value - high.astype(F32)).astype(jnp.bfloat16)
    return high, low


def spread_kernel(first, *refs):
    if first:
        (tiles, rows, cols, send, mask, source, in0, in1, in2, in3, parts,
         anchor, squared, out0, out1, out2, out3, own, operand, products) = refs
    else:
        (tiles, rows, cols, send, anchor, source, in0, in1, in2, in3, parts,
         squared, out0, out1, out2, out3, own, operand, products) = refs
    scale = scales(parts, 16)
    if first:
        seeded = jnp.concatenate(
            [mask[...].astype(F32), jnp.zeros((SIDE - 8, SIDE), F32)], axis=0
        )
        seeded = 64.0 * jnp.transpose(seeded)
    received = (in0, in1, in2, in3)
    for block in range(16):
        if block < 8:
            value = source[block]
        else:
            value = received[(block - 8) // 2][(block - 8) % 2]
        value = value * scale[:, block : block + 1]
        if first and block < 8:
            anchor[block] = seeded[:, block : block + 1] * value + 4.0
        high, low = split(value)
        operand[block, :SIDE, :] = high
        operand[block, SIDE:, :] = low
    odd = parity()
    for tile in range(32):
        weights = tiles[tile]
        products[tile] = jnp.dot(
            jnp.concatenate([weights, weights], axis=1),
            operand[buffer_block(cols[tile], odd)],
            preferred_element_type=F32,
        )
    squared[...] = anchor[...]
    for tile in range(32):
        row = rows[tile]
        squared[row] = squared[row] + products[tile]
    for block in range(8):
        value = squared[block]
        value = value * value
        squared[block] = value
        own[block : block + 1, :] = lane_sums(value)
    gather(squared, send, (out0, out1, out2, out3))


def last_kernel(squared, parts, out):
    scale = scales(parts, 8)
    for block in range(8):
        out[block] = squared[block] * scale[:, block : block + 1]


def exchange(outgoing):
    count = lax.axis_size("dom")
    targets = (
        lambda i: i ^ 1,
        lambda i: ((i + 1) ^ 1) - 1,
        lambda i: i + 2,
        lambda i: i - 2,
    )
    received = []
    for pair, target in zip(outgoing, targets):
        received.append(
            lax.ppermute(pair, "dom", [(i, target(i) % count) for i in range(count)])
        )
    return received


def on_device(tiles, tile_rows, tile_cols, send_lists, seed_mask, labels):
    blocks = labels.reshape(8, SIDE, SIDE)
    mask = seed_mask.reshape(8, SIDE)
    pairs = [shape(2, SIDE, SIDE)] * 4
    *outgoing, own = pl.pallas_call(
        first_kernel,
        out_shape=pairs + [shape(8, SIDE)],
        in_specs=[VMEM, SMEM],
        out_specs=[VMEM] * 5,
        compiler_params=PARAMS,
    )(blocks, send_lists)
    source = blocks
    anchor = None
    for iteration in range(ITERS):
        first = iteration == 0
        received = exchange(outgoing)
        parts = pl.pallas_call(
            mass_kernel,
            out_shape=shape(8, 16, SIDE),
            in_specs=[VMEM] * 5,
            out_specs=VMEM,
            compiler_params=PARAMS,
        )(own, *received)
        parts = lax.all_to_all(parts, "cls", 0, 0)
        results = pl.pallas_call(
            lambda *refs, first=first: spread_kernel(first, *refs),
            out_shape=[shape(8, SIDE, SIDE)] * (2 if first else 1) + pairs + [shape(8, SIDE)],
            in_specs=[VMEM, SMEM, SMEM, SMEM] + [VMEM] * 7,
            out_specs=[VMEM] * (7 if first else 6),
            scratch_shapes=[
                pltpu.VMEM((16, 2 * SIDE, SIDE), jnp.bfloat16),
                pltpu.VMEM((32, SIDE, SIDE), F32),
            ],
            compiler_params=PARAMS,
        )(tiles, tile_rows, tile_cols, send_lists, mask if first else anchor, source, *received, parts)
        if first:
            anchor, *results = results
        source, *outgoing, own = results
    parts = lax.all_to_all(jnp.broadcast_to(own[None], (8, 8, SIDE)), "cls", 0, 0)
    out = pl.pallas_call(
        last_kernel,
        out_shape=shape(8, SIDE, SIDE),
        in_specs=[VMEM, VMEM],
        out_specs=VMEM,
        compiler_params=PARAMS,
    )(source, parts)
    return out.reshape(8 * SIDE, SIDE)


def solution(mesh):
    return jax.shard_map(
        on_device,
        mesh=mesh,
        in_specs=(
            P("dom", None, None),
            P("dom"),
            P("dom"),
            P("dom", None, None),
            P("dom"),
            P("dom", "cls"),
        ),
        out_specs=P("dom", "cls"),
        check_vma=False,
    )
```

```python
import jax
import jax.numpy as jnp
from jax import lax
from jax.experimental import pallas as pl
from jax.experimental.pallas import tpu as pltpu
from jax.sharding import Mesh
from jax.sharding import PartitionSpec as P

CLASSES = 1024
ITERS = 3
SIDE = 128

VMEM = pl.BlockSpec(memory_space=pltpu.VMEM)
SMEM = pl.BlockSpec(memory_space=pltpu.SMEM)
F32 = jnp.float32
PARAMS = pltpu.CompilerParams(vmem_limit_bytes=16 * 1024 * 1024)


def shape(*dims):
    return jax.ShapeDtypeStruct(dims, F32)


def shift_right(value, by):
    return lax.shift_right_logical(value, by)


def gather(source, send, out0, out1):
    odd = lax.rem(lax.axis_index("chip"), 2)
    for out, behind in ((out0, odd), (out1, 1 - odd)):
        for part in range(2):
            slot = 2 * behind + 1 - part
            for within in range(2):
                out[2 * part + within] = source[send[0, slot, within]]


def operand_block(col):
    odd = lax.rem(lax.axis_index("chip"), 2)
    core = lax.axis_index("core")
    ghost = jnp.maximum(col - 8, 0)
    offset = shift_right(ghost, 1)
    half = shift_right(offset, 1)
    near = half ^ (1 - core)
    far = 2 + (half ^ (1 - odd))
    pair = jnp.where(lax.rem(offset, 2) == 1, far, near)
    return jnp.where(col < 8, col, 8 + 2 * pair + lax.rem(ghost, 2))


def lane_sums(block):
    return jnp.sum(jnp.transpose(block), axis=0, keepdims=True)


def first_kernel(labels, rows, cols, send, mask, kept, out0, out1, own):
    gather(labels, send, out0, out1)
    for block in range(8):
        kept[block] = labels[block]
        own[block : block + 1, :] = lane_sums(labels[block])


def mass_kernel(send, source, own, in0, in1, parts, relay, rows):
    odd = lax.rem(lax.axis_index("chip"), 2)
    core = lax.axis_index("core")
    rows[0:8, :] = own[...]
    for within in range(2):
        block = send[0, 2 * core, within]
        relay[within] = source[block]
        rows[12 + within : 13 + within, :] = own[pl.ds(block, 1), :]
        rows[8 + within : 9 + within, :] = lane_sums(in0[within])
        rows[10 + within : 11 + within, :] = lane_sums(in1[within])

    def pass_on(received):
        for within in range(2):
            value = received[2 + within]
            relay[2 + within] = value
            rows[14 + within : 15 + within, :] = lane_sums(value)

    pl.when(odd == core)(lambda: pass_on(in0))
    pl.when(odd != core)(lambda: pass_on(in1))
    partial = rows[...]
    for share in range(16):
        parts[share] = partial


def scales(total, blocks):
    scale = CLASSES / total
    full = jnp.concatenate([scale, jnp.zeros((SIDE - blocks, SIDE), F32)], axis=0)
    return jnp.transpose(full)


def total_of(parts, core):
    total = parts[8 * core]
    for share in range(1, 8):
        total = total + parts[8 * core + share]
    return total


def split(value):
    high = value.astype(jnp.bfloat16)
    low = (value - high.astype(F32)).astype(jnp.bfloat16)
    return high, low


def spread_kernel(first, last, *refs):
    refs = list(refs)
    tiles, rows, cols, send, mask, source, in0, in1, near, parts = refs[:10]
    refs = refs[10:]
    anchor = refs.pop(0) if first else mask
    squared = refs.pop(0)
    if last:
        own_parts, operand, products = refs
    else:
        out0, out1, own, operand, products = refs
    core = lax.axis_index("core")
    mine = total_of(parts, core)
    mate = total_of(parts, 1 - core)
    scale = scales(jnp.concatenate([mine[0:8], mate[12:16], mine[8:12]], axis=0), 16)
    if first:
        seeded = jnp.concatenate(
            [mask[...].astype(F32), jnp.zeros((SIDE - 8, SIDE), F32)], axis=0
        )
        seeded = 64.0 * jnp.transpose(seeded)
    blocks = [(source, block) for block in range(8)]
    blocks += [(near, block) for block in range(4)]
    blocks += [(in0, 0), (in0, 1), (in1, 0), (in1, 1)]
    for block, (ref, place) in enumerate(blocks):
        value = ref[place] * scale[:, block : block + 1]
        if first and block < 8:
            anchor[block] = seeded[:, block : block + 1] * value + 4.0
        high, low = split(value)
        operand[block, :SIDE, :] = high
        operand[block, SIDE:, :] = low
    for tile in range(32):
        weights = tiles[tile]
        products[tile] = jnp.dot(
            jnp.concatenate([weights, weights], axis=1),
            operand[operand_block(cols[tile])],
            preferred_element_type=F32,
        )
    squared[...] = anchor[...]
    for tile in range(32):
        row = rows[tile]
        squared[row] = squared[row] + products[tile]
    sums = []
    for block in range(8):
        value = squared[block]
        value = value * value
        squared[block] = value
        sums.append(lane_sums(value))
    sums = jnp.concatenate(sums, axis=0)
    if last:
        for share in range(8):
            own_parts[share] = sums
    else:
        own[...] = sums
        gather(squared, send, out0, out1)


def last_kernel(squared, parts, out):
    scale = scales(total_of(parts, 0), 8)
    for block in range(8):
        out[block] = squared[block] * scale[:, block : block + 1]


def on_device(tiles, tile_rows, tile_cols, send_lists, seed_mask, labels):
    chips = lax.axis_size("chip")
    first_swap = [(i, i ^ 1) for i in range(chips)]
    second_swap = [(i, (((i + 1) ^ 1) - 1) % chips) for i in range(chips)]
    blocks = labels.reshape(8, SIDE, SIDE)
    mask = seed_mask.reshape(8, SIDE)
    own_shape = shape(8, SIDE, SIDE)
    swap_shape = shape(4, SIDE, SIDE)
    source, out0, out1, own = pl.pallas_call(
        first_kernel,
        out_shape=[own_shape, swap_shape, swap_shape, shape(8, SIDE)],
        in_specs=[VMEM, SMEM, SMEM, SMEM, VMEM],
        out_specs=[VMEM] * 4,
        compiler_params=PARAMS,
    )(blocks, tile_rows, tile_cols, send_lists, mask)
    anchor = None
    for iteration in range(ITERS):
        first = iteration == 0
        last = iteration == ITERS - 1
        in0 = lax.ppermute(out0, "chip", first_swap)
        in1 = lax.ppermute(out1, "chip", second_swap)
        parts, relay = pl.pallas_call(
            mass_kernel,
            out_shape=[shape(16, 16, SIDE), swap_shape],
            in_specs=[SMEM] + [VMEM] * 4,
            out_specs=[VMEM, VMEM],
            scratch_shapes=[pltpu.VMEM((16, SIDE), F32)],
            compiler_params=PARAMS,
        )(send_lists, source, own, in0, in1)
        near = lax.ppermute(relay, "core", [(0, 1), (1, 0)])
        parts = lax.all_to_all(parts, ("core", "cls"), 0, 0)
        out_shape = [own_shape] * (2 if first else 1)
        out_shape += [shape(8, 8, SIDE)] if last else [swap_shape, swap_shape, shape(8, SIDE)]
        results = pl.pallas_call(
            lambda *refs, first=first, last=last: spread_kernel(first, last, *refs),
            out_shape=out_shape,
            in_specs=[VMEM, SMEM, SMEM, SMEM] + [VMEM] * 6,
            out_specs=[VMEM] * len(out_shape),
            scratch_shapes=[
                pltpu.VMEM((16, 2 * SIDE, SIDE), jnp.bfloat16),
                pltpu.VMEM((32, SIDE, SIDE), F32),
            ],
            compiler_params=PARAMS,
        )(tiles, tile_rows, tile_cols, send_lists, mask if first else anchor, source, in0, in1, near, parts)
        if first:
            anchor, *results = results
        if last:
            source, parts = results
        else:
            source, out0, out1, own = results
    parts = lax.all_to_all(parts, "cls", 0, 0)
    out = pl.pallas_call(
        last_kernel,
        out_shape=own_shape,
        in_specs=[VMEM, VMEM],
        out_specs=VMEM,
        compiler_params=PARAMS,
    )(source, parts)
    return out.reshape(8 * SIDE, SIDE)


def solution(mesh):
    split_mesh = Mesh(
        mesh.devices.reshape(mesh.shape["dom"] // 2, 2, mesh.shape["cls"]), ("chip", "core", "cls")
    )
    dom = ("chip", "core")
    return jax.shard_map(
        on_device,
        mesh=split_mesh,
        in_specs=(P(dom, None, None), P(dom), P(dom), P(dom, None, None), P(dom), P(dom, "cls")),
        out_specs=P(dom, "cls"),
        check_vma=False,
    )
```

```python
import jax
import jax.numpy as jnp
from jax import lax
from jax.experimental import pallas as pl
from jax.experimental.pallas import tpu as pltpu
from jax.sharding import Mesh
from jax.sharding import PartitionSpec as P

CLASSES = 1024
ITERS = 3
SIDE = 128

VMEM = pl.BlockSpec(memory_space=pltpu.VMEM)
SMEM = pl.BlockSpec(memory_space=pltpu.SMEM)
F32 = jnp.float32
PARAMS = pltpu.CompilerParams(vmem_limit_bytes=16 * 1024 * 1024)


def shape(*dims):
    return jax.ShapeDtypeStruct(dims, F32)


def shift_right(value, by):
    return lax.shift_right_logical(value, by)


def sent_blocks(send, outs):
    odd = lax.rem(lax.axis_index("chip"), 2)
    for out, behind in zip(outs, (odd, 1 - odd)):
        for part in range(2):
            for within in range(2):
                yield out, 2 * part + within, send[0, within, 2 * behind + 1 - part]


def gather(source, send, outs):
    for out, place, block in sent_blocks(send, outs):
        out[place] = source[block]


def operand_block(col):
    odd = lax.rem(lax.axis_index("chip"), 2)
    core = lax.axis_index("core")
    ghost = jnp.maximum(col - 8, 0)
    offset = shift_right(ghost, 1)
    half = shift_right(offset, 1)
    near = half ^ (1 - core)
    far = 2 + (half ^ (1 - odd))
    pair = jnp.where(lax.rem(offset, 2) == 1, far, near)
    return jnp.where(col < 8, col, 8 + 2 * pair + lax.rem(ghost, 2))


def lane_sums(block):
    return jnp.sum(jnp.transpose(block), axis=0, keepdims=True)


def fetch_kernel(labels, send, out0, out1, sems):
    copies = []
    for number, (out, place, block) in enumerate(sent_blocks(send, (out0, out1))):
        copy = pltpu.make_async_copy(labels.at[block], out.at[place], sems.at[number])
        copy.start()
        copies.append(copy)
    for copy in copies:
        copy.wait()


def fill_parts(sums, send, parts, rows):
    rows[0:8, :] = sums
    rows[8:16, :] = jnp.zeros((8, SIDE), F32)
    for half in range(2):
        for within in range(2):
            place = 8 + 2 * half + within
            rows[place : place + 1, :] = rows[pl.ds(send[0, within, 2 * half], 1), :]
    partial = rows[...]
    for share in range(16):
        parts[share] = partial


def first_kernel(labels, rows, cols, send, mask, kept, parts, scratch):
    sums = []
    for block in range(8):
        value = labels[block]
        kept[block] = value
        sums.append(lane_sums(value))
    fill_parts(jnp.concatenate(sums, axis=0), send, parts, scratch)


def mass_kernel(parts, send, source, in0, in1, known, mass0, mass1, relay):
    odd = lax.rem(lax.axis_index("chip"), 2)
    core = lax.axis_index("core")
    mine = total_of(parts, core)
    mate = total_of(parts, 1 - core)
    known[0:8, :] = mine[0:8]
    known[8:10, :] = jnp.where(core == 0, mate[10:12], mate[8:10])
    known[10:16, :] = jnp.ones((6, SIDE), F32)
    for out, behind in ((mass0, odd), (mass1, 1 - odd)):
        for within in range(2):
            block = send[0, within, 2 * behind + 1]
            out[within : within + 1, :] = known[pl.ds(block, 1), :]
        out[2:4, :] = jnp.where(behind == 0, mate[8:10], mate[10:12])
        out[4:8, :] = jnp.ones((4, SIDE), F32)
    for within in range(2):
        relay[within] = source[send[0, within, 2 * core]]

    def pass_on(received):
        for within in range(2):
            relay[2 + within] = received[2 + within]

    pl.when(odd == core)(lambda: pass_on(in0))
    pl.when(odd != core)(lambda: pass_on(in1))


def scales(total, blocks):
    scale = CLASSES / total
    full = jnp.concatenate([scale, jnp.zeros((SIDE - blocks, SIDE), F32)], axis=0)
    return jnp.transpose(full)


def total_of(parts, core):
    total = parts[8 * core]
    for share in range(1, 8):
        total = total + parts[8 * core + share]
    return total


def split(value):
    high = value.astype(jnp.bfloat16)
    low = (value - high.astype(F32)).astype(jnp.bfloat16)
    return high, low


def spread_kernel(first, last, *refs):
    refs = list(refs)
    tiles, rows, cols, send, mask, source, in0, in1, near, known, mass0, mass1 = refs[:12]
    refs = refs[12:]
    anchor = refs.pop(0) if first else mask
    squared = refs.pop(0)
    if last:
        parts, operand, products = refs
    else:
        out0, out1, parts, operand, products, scratch = refs
    odd = lax.rem(lax.axis_index("chip"), 2)
    core = lax.axis_index("core")
    relayed = jnp.where(odd != core, mass0[2:4, :], mass1[2:4, :])
    total = jnp.concatenate([known[0:10, :], relayed, mass0[0:2, :], mass1[0:2, :]], axis=0)
    scale = scales(total, 16)
    if first:
        seeded = jnp.concatenate(
            [mask[...].astype(F32), jnp.zeros((SIDE - 8, SIDE), F32)], axis=0
        )
        seeded = 64.0 * jnp.transpose(seeded)
    blocks = [(source, block) for block in range(8)]
    blocks += [(near, block) for block in range(4)]
    blocks += [(in0, 0), (in0, 1), (in1, 0), (in1, 1)]
    for block, (ref, place) in enumerate(blocks):
        value = ref[place] * scale[:, block : block + 1]
        if first and block < 8:
            anchor[block] = seeded[:, block : block + 1] * value + 4.0
        high, low = split(value)
        operand[block, :SIDE, :] = high
        operand[block, SIDE:, :] = low
    for tile in range(32):
        weights = tiles[tile]
        products[tile] = jnp.dot(
            jnp.concatenate([weights, weights], axis=1),
            operand[operand_block(cols[tile])],
            preferred_element_type=F32,
        )
    squared[...] = anchor[...]
    for tile in range(32):
        row = rows[tile]
        squared[row] = squared[row] + products[tile]
    sums = []
    for block in range(8):
        value = squared[block]
        value = value * value
        squared[block] = value
        sums.append(lane_sums(value))
    sums = jnp.concatenate(sums, axis=0)
    if last:
        for share in range(8):
            parts[share] = sums
    else:
        gather(squared, send, (out0, out1))
        fill_parts(sums, send, parts, scratch)


def last_kernel(squared, parts, out):
    scale = scales(total_of(parts, 0), 8)
    for block in range(8):
        out[block] = squared[block] * scale[:, block : block + 1]


def on_device(tiles, tile_rows, tile_cols, send_lists, seed_mask, labels):
    chips = lax.axis_size("chip")
    first_swap = [(i, i ^ 1) for i in range(chips)]
    second_swap = [(i, (((i + 1) ^ 1) - 1) % chips) for i in range(chips)]
    send_lists = jnp.transpose(send_lists, (0, 2, 1))
    blocks = labels.reshape(8, SIDE, SIDE)
    mask = seed_mask.reshape(8, SIDE)
    own_shape = shape(8, SIDE, SIDE)
    swap_shape = shape(4, SIDE, SIDE)
    parts_shape = shape(16, 16, SIDE)
    rows_scratch = pltpu.VMEM((16, SIDE), F32)
    out0, out1 = pl.pallas_call(
        fetch_kernel,
        out_shape=[swap_shape, swap_shape],
        in_specs=[pl.BlockSpec(memory_space=pltpu.HBM), SMEM],
        out_specs=[VMEM] * 2,
        scratch_shapes=[pltpu.SemaphoreType.DMA((8,))],
        compiler_params=PARAMS,
        cost_estimate=pl.CostEstimate(flops=0, bytes_accessed=1 << 19, transcendentals=0),
    )(blocks, send_lists)
    source, parts = pl.pallas_call(
        first_kernel,
        out_shape=[own_shape, parts_shape],
        in_specs=[VMEM, SMEM, SMEM, SMEM, VMEM],
        out_specs=[VMEM] * 2,
        scratch_shapes=[rows_scratch],
        compiler_params=PARAMS,
        cost_estimate=pl.CostEstimate(flops=1 << 20, bytes_accessed=1 << 20, transcendentals=0),
    )(blocks, tile_rows, tile_cols, send_lists, mask)
    anchor = None
    for iteration in range(ITERS):
        first = iteration == 0
        last = iteration == ITERS - 1
        in0 = lax.ppermute(out0, "chip", first_swap)
        in1 = lax.ppermute(out1, "chip", second_swap)
        parts = lax.all_to_all(parts, ("core", "cls"), 0, 0)
        known, mass0, mass1, relay = pl.pallas_call(
            mass_kernel,
            out_shape=[shape(16, SIDE), shape(8, SIDE), shape(8, SIDE), swap_shape],
            in_specs=[VMEM, SMEM] + [VMEM] * 3,
            out_specs=[VMEM] * 4,
            compiler_params=PARAMS,
        )(parts, send_lists, source, in0, in1)
        near = lax.ppermute(relay, "core", [(0, 1), (1, 0)])
        mass0 = lax.ppermute(mass0, "chip", first_swap)
        mass1 = lax.ppermute(mass1, "chip", second_swap)
        out_shape = [own_shape] * (2 if first else 1)
        out_shape += [shape(8, 8, SIDE)] if last else [swap_shape, swap_shape, parts_shape]
        results = pl.pallas_call(
            lambda *refs, first=first, last=last: spread_kernel(first, last, *refs),
            out_shape=out_shape,
            in_specs=[VMEM, SMEM, SMEM, SMEM] + [VMEM] * 8,
            out_specs=[VMEM] * len(out_shape),
            scratch_shapes=[
                pltpu.VMEM((16, 2 * SIDE, SIDE), jnp.bfloat16),
                pltpu.VMEM((32, SIDE, SIDE), F32),
            ]
            + ([] if last else [rows_scratch]),
            compiler_params=PARAMS,
            cost_estimate=pl.CostEstimate(flops=1 << 28, bytes_accessed=1 << 22, transcendentals=0),
        )(
            tiles, tile_rows, tile_cols, send_lists, mask if first else anchor, source,
            in0, in1, near, known, mass0, mass1,
        )
        if first:
            anchor, *results = results
        if last:
            source, parts = results
        else:
            source, out0, out1, parts = results
    parts = lax.all_to_all(parts, "cls", 0, 0)
    out = pl.pallas_call(
        last_kernel,
        out_shape=own_shape,
        in_specs=[VMEM, VMEM],
        out_specs=VMEM,
        compiler_params=PARAMS,
    )(source, parts)
    return out.reshape(8 * SIDE, SIDE)


def solution(mesh):
    split_mesh = Mesh(
        mesh.devices.reshape(mesh.shape["dom"] // 2, 2, mesh.shape["cls"]), ("chip", "core", "cls")
    )
    dom = ("chip", "core")
    return jax.shard_map(
        on_device,
        mesh=split_mesh,
        in_specs=(P(dom, None, None), P(dom), P(dom), P(dom, None, None), P(dom), P(dom, "cls")),
        out_specs=P(dom, "cls"),
        check_vma=False,
    )
```

```python
import jax
import jax.numpy as jnp
from jax import lax
from jax.experimental import pallas as pl
from jax.experimental.pallas import tpu as pltpu
from jax.sharding import Mesh
from jax.sharding import PartitionSpec as P

CLASSES = 1024
ITERS = 3
SIDE = 128

VMEM = pl.BlockSpec(memory_space=pltpu.VMEM)
SMEM = pl.BlockSpec(memory_space=pltpu.SMEM)
HBM = pl.BlockSpec(memory_space=pltpu.HBM)
F32 = jnp.float32
PARAMS = pltpu.CompilerParams(vmem_limit_bytes=16 * 1024 * 1024)


def shape(*dims):
    return jax.ShapeDtypeStruct(dims, F32)


def shift_right(value, by):
    return lax.shift_right_logical(value, by)


def previous_first():
    return 1 - lax.rem(lax.axis_index("chip"), 2)


def plan_entries(rows, cols, send):
    core = lax.axis_index("core")
    for tile in range(32):
        yield rows[tile]
    for tile in range(32):
        col = cols[tile]
        ghost = jnp.maximum(col - 8, 0)
        offset = shift_right(ghost, 1)
        half = shift_right(offset, 1)
        near = half ^ (1 - core)
        far = 2 + (half ^ (1 - previous_first()))
        pair = jnp.where(lax.rem(offset, 2) == 1, far, near)
        yield jnp.where(col < 8, col, 8 + 2 * pair + lax.rem(ghost, 2))
    for offset in range(4):
        for within in range(2):
            yield send[0, within, offset]


def row_block(plan, tile):
    return plan[tile]


def operand_block(plan, tile):
    return plan[32 + tile]


def sent_block(plan, offset, within):
    return plan[64 + 2 * offset + within]


def block_at(ref, place):
    return ref[SIDE * place : SIDE * (place + 1), :]


def fill_swaps(source, sums, plan, outs):
    previous = previous_first()
    for out, behind in zip(outs, (previous, 1 - previous)):
        out[4 * SIDE + 4 :, :] = jnp.zeros((4, SIDE), F32)
        for part in range(2):
            for within in range(2):
                place = 2 * part + within
                block = sent_block(plan, 2 * behind + 1 - part, within)
                out[SIDE * place : SIDE * (place + 1), :] = source[block]
                out[4 * SIDE + place : 4 * SIDE + place + 1, :] = sums[pl.ds(block, 1), :]


def lane_sums(block):
    return jnp.sum(jnp.transpose(block), axis=0, keepdims=True)


def first_kernel(labels, rows, cols, send, mask, kept, mask_kept, plan, out0, out1, own, *scratch):
    rows_here, cols_here, send_here, sems = scratch
    pairs = [(rows, rows_here), (cols, cols_here), (send, send_here)]
    pairs += [(labels.at[block], kept.at[block]) for block in range(8)]
    pairs += [(mask, mask_kept)]
    copies = []
    for number, (here, there) in enumerate(pairs):
        copy = pltpu.make_async_copy(here, there, sems.at[number])
        copy.start()
        copies.append(copy)
    for copy in copies[:3]:
        copy.wait()
    for place, entry in enumerate(plan_entries(rows_here, cols_here, send_here)):
        plan[place] = entry
    for block in range(8):
        copies[3 + block].wait()
        own[block : block + 1, :] = lane_sums(kept[block])
    fill_swaps(kept, own, plan, (out0, out1))
    copies[11].wait()


def mass_kernel(plan, source, own, in0, in1, parts, relay, rows):
    previous = previous_first()
    core = lax.axis_index("core")
    rows[0:8, :] = own[...]
    rows[8:10, :] = in0[4 * SIDE : 4 * SIDE + 2, :]
    rows[10:12, :] = in1[4 * SIDE : 4 * SIDE + 2, :]
    for within in range(2):
        block = sent_block(plan, 2 * core, within)
        relay[within] = source[block]
        rows[12 + within : 13 + within, :] = own[pl.ds(block, 1), :]

    def pass_on(received):
        for within in range(2):
            relay[2 + within] = block_at(received, 2 + within)
        rows[14:16, :] = received[4 * SIDE + 2 : 4 * SIDE + 4, :]

    pl.when(previous == core)(lambda: pass_on(in0))
    pl.when(previous != core)(lambda: pass_on(in1))
    partial = rows[...]
    for share in range(16):
        parts[share] = partial


def scales(total, blocks):
    scale = CLASSES / total
    full = jnp.concatenate([scale, jnp.zeros((SIDE - blocks, SIDE), F32)], axis=0)
    return jnp.transpose(full)


def total_of(parts, core):
    total = parts[8 * core]
    for share in range(1, 8):
        total = total + parts[8 * core + share]
    return total


def split(value):
    high = value.astype(jnp.bfloat16)
    low = (value - high.astype(F32)).astype(jnp.bfloat16)
    return high, low


def spread_kernel(first, last, *refs):
    refs = list(refs)
    tiles, plan, mask, source, in0, in1, near, parts = refs[:8]
    refs = refs[8:]
    anchor = refs.pop(0) if first else mask
    squared = refs.pop(0)
    if last:
        own_parts, operand, products = refs
    else:
        out0, out1, own, operand, products = refs
    core = lax.axis_index("core")
    mine = total_of(parts, core)
    mate = total_of(parts, 1 - core)
    scale = scales(jnp.concatenate([mine[0:8], mate[12:16], mine[8:12]], axis=0), 16)
    if first:
        seeded = jnp.concatenate(
            [mask[...].astype(F32), jnp.zeros((SIDE - 8, SIDE), F32)], axis=0
        )
        seeded = 64.0 * jnp.transpose(seeded)
    for block in range(16):
        if block < 8:
            value = source[block]
        elif block < 12:
            value = near[block - 8]
        else:
            value = block_at(in0 if block < 14 else in1, block % 2)
        value = value * scale[:, block : block + 1]
        if first and block < 8:
            anchor[block] = seeded[:, block : block + 1] * value + 4.0
        high, low = split(value)
        operand[block, :SIDE, :] = high
        operand[block, SIDE:, :] = low
    for tile in range(32):
        weights = tiles[tile]
        products[tile] = jnp.dot(
            jnp.concatenate([weights, weights], axis=1),
            operand[operand_block(plan, tile)],
            preferred_element_type=F32,
        )
    squared[...] = anchor[...]
    for tile in range(32):
        row = row_block(plan, tile)
        squared[row] = squared[row] + products[tile]
    sums = []
    for block in range(8):
        value = squared[block]
        value = value * value
        squared[block] = value
        sums.append(lane_sums(value))
    sums = jnp.concatenate(sums, axis=0)
    if last:
        for share in range(8):
            own_parts[share] = sums
    else:
        own[...] = sums
        fill_swaps(squared, own, plan, (out0, out1))


def last_kernel(squared, parts, out):
    scale = scales(total_of(parts, 0), 8)
    for block in range(8):
        out[block] = squared[block] * scale[:, block : block + 1]


def on_device(tiles, tile_rows, tile_cols, send_lists, seed_mask, labels):
    chips = lax.axis_size("chip")
    swap0 = [(i, (((i + 1) ^ 1) - 1) % chips) for i in range(chips)]
    swap1 = [(i, i ^ 1) for i in range(chips)]
    send_lists = jnp.transpose(send_lists, (0, 2, 1))
    blocks = labels.reshape(8, SIDE, SIDE)
    mask = seed_mask.reshape(8, SIDE)
    own_shape = shape(8, SIDE, SIDE)
    swap_shape = shape(4 * SIDE + 8, SIDE)
    source, mask, plan, out0, out1, own = pl.pallas_call(
        first_kernel,
        out_shape=[
            own_shape,
            jax.ShapeDtypeStruct((8, SIDE), jnp.int32),
            jax.ShapeDtypeStruct((72,), jnp.int32),
            swap_shape,
            swap_shape,
            shape(8, SIDE),
        ],
        in_specs=[HBM] * 5,
        out_specs=[VMEM, VMEM, SMEM, VMEM, VMEM, VMEM],
        scratch_shapes=[
            pltpu.SMEM((32,), jnp.int32),
            pltpu.SMEM((32,), jnp.int32),
            pltpu.SMEM((1, 2, 4), jnp.int32),
            pltpu.SemaphoreType.DMA((12,)),
        ],
        compiler_params=PARAMS,
    )(*[
        pltpu.with_memory_space_constraint(value, pltpu.HBM)
        for value in (blocks, tile_rows, tile_cols, send_lists, mask)
    ])
    anchor = None
    for iteration in range(ITERS):
        first = iteration == 0
        last = iteration == ITERS - 1
        in0 = lax.ppermute(out0, "chip", swap0)
        in1 = lax.ppermute(out1, "chip", swap1)
        parts, relay = pl.pallas_call(
            mass_kernel,
            out_shape=[shape(16, 16, SIDE), shape(4, SIDE, SIDE)],
            in_specs=[SMEM] + [VMEM] * 4,
            out_specs=[VMEM, VMEM],
            scratch_shapes=[pltpu.VMEM((16, SIDE), F32)],
            compiler_params=PARAMS,
        )(plan, source, own, in0, in1)
        near = lax.ppermute(relay, "core", [(0, 1), (1, 0)])
        parts = lax.all_to_all(parts, ("core", "cls"), 0, 0)
        out_shape = [own_shape] * (2 if first else 1)
        out_shape += [shape(8, 8, SIDE)] if last else [swap_shape, swap_shape, shape(8, SIDE)]
        results = pl.pallas_call(
            lambda *refs, first=first, last=last: spread_kernel(first, last, *refs),
            out_shape=out_shape,
            in_specs=[VMEM, SMEM] + [VMEM] * 6,
            out_specs=[VMEM] * len(out_shape),
            scratch_shapes=[
                pltpu.VMEM((16, 2 * SIDE, SIDE), jnp.bfloat16),
                pltpu.VMEM((32, SIDE, SIDE), F32),
            ],
            compiler_params=PARAMS,
        )(tiles, plan, mask if first else anchor, source, in0, in1, near, parts)
        if first:
            anchor, *results = results
        if last:
            source, parts = results
        else:
            source, out0, out1, own = results
    parts = lax.all_to_all(parts, "cls", 0, 0)
    out = pl.pallas_call(
        last_kernel,
        out_shape=own_shape,
        in_specs=[VMEM, VMEM],
        out_specs=VMEM,
        compiler_params=PARAMS,
    )(source, parts)
    return out.reshape(8 * SIDE, SIDE)


def solution(mesh):
    split_mesh = Mesh(
        mesh.devices.reshape(mesh.shape["dom"] // 2, 2, mesh.shape["cls"]), ("chip", "core", "cls")
    )
    dom = ("chip", "core")
    return jax.shard_map(
        on_device,
        mesh=split_mesh,
        in_specs=(P(dom, None, None), P(dom), P(dom), P(dom, None, None), P(dom), P(dom, "cls")),
        out_specs=P(dom, "cls"),
        check_vma=False,
    )
```

```python
import functools

import jax
import jax.numpy as jnp
from jax import lax
from jax.experimental import pallas as pl
from jax.experimental.pallas import tpu as pltpu
from jax.sharding import Mesh
from jax.sharding import PartitionSpec as P

CLASSES = 1024
ITERS = 3
SIDE = 128

VMEM = pl.BlockSpec(memory_space=pltpu.VMEM)
SMEM = pl.BlockSpec(memory_space=pltpu.SMEM)
HBM = pl.BlockSpec(memory_space=pltpu.HBM)
F32 = jnp.float32
PARAMS = pltpu.CompilerParams(vmem_limit_bytes=16 * 1024 * 1024)


def shape(*dims):
    return jax.ShapeDtypeStruct(dims, F32)


def shift_right(value, by):
    return lax.shift_right_logical(value, by)


def plan_entries(rows, cols, send):
    core = lax.axis_index("core")
    for tile in range(32):
        yield rows[tile]
    for tile in range(32):
        col = cols[tile]
        ghost = jnp.maximum(col - 8, 0)
        offset = shift_right(ghost, 1)
        half = shift_right(offset, 1)
        pair = jnp.where(lax.rem(offset, 2) == 1, 2 + (half ^ (1 - core)), half ^ core)
        yield jnp.where(col < 8, col, 8 + 2 * pair + lax.rem(ghost, 2))
    for offset in range(4):
        for within in range(2):
            yield send[0, within, offset]


def row_block(plan, tile):
    return plan[tile]


def operand_block(plan, tile):
    return plan[32 + tile]


def sent_block(plan, offset, within):
    return plan[64 + 2 * offset + within]


def block_at(ref, place):
    return ref[SIDE * place : SIDE * (place + 1), :]


def fill_swaps(source, sums, block_of, wide, narrow):
    core = lax.axis_index("core")
    for out, offsets in ((wide, (2 - 2 * core, 3 - 2 * core)), (narrow, (1 + 2 * core,))):
        count = 2 * len(offsets)
        out[count * SIDE + count :, :] = jnp.zeros((8 - count, SIDE), F32)
        for part, offset in enumerate(offsets):
            for within in range(2):
                place = 2 * part + within
                block = block_of(offset, within)
                out[SIDE * place : SIDE * (place + 1), :] = source[block]
                out[count * SIDE + place : count * SIDE + place + 1, :] = sums[pl.ds(block, 1), :]


def lane_sums(block):
    return jnp.sum(jnp.transpose(block), axis=0, keepdims=True)


def copy_all(pairs, sems):
    copies = []
    for number, (here, there) in enumerate(pairs):
        copy = pltpu.make_async_copy(here, there, sems.at[number])
        copy.start()
        copies.append(copy)
    return copies


def first_kernel(labels, send, kept, wide, narrow, own, send_here, sems):
    pairs = [(labels.at[block], kept.at[block]) for block in range(8)]
    copies = copy_all([(send, send_here)] + pairs, sems)
    for block in range(8):
        copies[1 + block].wait()
        own[block : block + 1, :] = lane_sums(kept[block])
    copies[0].wait()
    fill_swaps(kept, own, lambda offset, within: send_here[0, within, offset], wide, narrow)


def plan_kernel(rows, cols, send, mask, plan, mask_kept, rows_here, cols_here, send_here, sems):
    copies = copy_all([(rows, rows_here), (cols, cols_here), (send, send_here), (mask, mask_kept)], sems)
    for copy in copies:
        copy.wait()
    for place, entry in enumerate(plan_entries(rows_here, cols_here, send_here)):
        plan[place] = entry


def mass_kernel(plan, source, own, wide, narrow, parts, relay, rows):
    core = lax.axis_index("core")
    rows[0:8, :] = own[...]
    rows[8:10, :] = wide[4 * SIDE : 4 * SIDE + 2, :]
    rows[12:14, :] = wide[4 * SIDE + 2 : 4 * SIDE + 4, :]
    rows[14:16, :] = narrow[2 * SIDE : 2 * SIDE + 2, :]
    for within in range(2):
        block = sent_block(plan, 2 * core, within)
        rows[10 + within : 11 + within, :] = own[pl.ds(block, 1), :]
        relay[within] = source[block]
        relay[2 + within] = block_at(wide, 2 + within)
        relay[4 + within] = block_at(narrow, within)
    partial = rows[...]
    for share in range(16):
        parts[share] = partial


def scales(total, blocks):
    scale = CLASSES / total
    full = jnp.concatenate([scale, jnp.zeros((SIDE - blocks, SIDE), F32)], axis=0)
    return jnp.transpose(full)


def total_of(parts, core):
    total = parts[8 * core]
    for share in range(1, 8):
        total = total + parts[8 * core + share]
    return total


def split(value):
    high = value.astype(jnp.bfloat16)
    low = (value - high.astype(F32)).astype(jnp.bfloat16)
    return high, low


def spread_kernel(first, last, *refs):
    refs = list(refs)
    tiles, plan, mask, source, wide, relay, parts = refs[:7]
    refs = refs[7:]
    anchor = refs.pop(0) if first else mask
    squared = refs.pop(0)
    if last:
        own_parts, operand, products = refs
    else:
        wide_out, narrow_out, own, operand, products = refs
    core = lax.axis_index("core")
    mine = total_of(parts, core)
    mate = total_of(parts, 1 - core)
    scale = scales(jnp.concatenate([mine[0:10], mate[10:16]], axis=0), 16)
    if first:
        seeded = jnp.concatenate(
            [mask[...].astype(F32), jnp.zeros((SIDE - 8, SIDE), F32)], axis=0
        )
        seeded = 64.0 * jnp.transpose(seeded)
    for block in range(16):
        if block < 8:
            value = source[block]
        elif block < 10:
            value = block_at(wide, block - 8)
        else:
            value = relay[block - 10]
        value = value * scale[:, block : block + 1]
        if first and block < 8:
            anchor[block] = seeded[:, block : block + 1] * value + 4.0
        high, low = split(value)
        operand[block, :SIDE, :] = high
        operand[block, SIDE:, :] = low
    for tile in range(32):
        weights = tiles[tile]
        products[tile] = jnp.dot(
            jnp.concatenate([weights, weights], axis=1),
            operand[operand_block(plan, tile)],
            preferred_element_type=F32,
        )
    squared[...] = anchor[...]
    for tile in range(32):
        row = row_block(plan, tile)
        squared[row] = squared[row] + products[tile]
    sums = []
    for block in range(8):
        value = squared[block]
        value = value * value
        squared[block] = value
        sums.append(lane_sums(value))
    sums = jnp.concatenate(sums, axis=0)
    if last:
        for share in range(8):
            own_parts[share] = sums
    else:
        own[...] = sums
        block_of = functools.partial(sent_block, plan)
        fill_swaps(squared, own, block_of, wide_out, narrow_out)


def last_kernel(squared, parts, out, scaled, sems):
    scale = scales(total_of(parts, 0), 8)
    copies = []
    for block in range(8):
        scaled[block] = squared[block] * scale[:, block : block + 1]
        copy = pltpu.make_async_copy(scaled.at[block], out.at[block], sems.at[block])
        copy.start()
        copies.append(copy)
    for copy in copies:
        copy.wait()


def on_device(tiles, tile_rows, tile_cols, send_lists, seed_mask, labels):
    dom = ("chip", "core")
    count = 2 * lax.axis_size("chip")
    adjacent = [(i, (i + (1 if i % 2 else -1)) % count) for i in range(count)]
    three_away = [(i, (i + (-3 if i % 2 else 3)) % count) for i in range(count)]
    send_lists = jnp.transpose(send_lists, (0, 2, 1))
    own_shape = shape(8, SIDE, SIDE)
    swap_shapes = [shape(4 * SIDE + 8, SIDE), shape(2 * SIDE + 8, SIDE), shape(8, SIDE)]
    blocks, tile_rows, tile_cols, send_lists, mask = [
        pltpu.with_memory_space_constraint(value, pltpu.HBM)
        for value in (
            labels.reshape(8, SIDE, SIDE),
            tile_rows,
            tile_cols,
            send_lists,
            seed_mask.reshape(8, SIDE),
        )
    ]
    send_scratch = pltpu.SMEM((1, 2, 4), jnp.int32)
    source, wide, narrow, own = pl.pallas_call(
        first_kernel,
        out_shape=[own_shape] + swap_shapes,
        in_specs=[HBM] * 2,
        out_specs=[VMEM] * 4,
        scratch_shapes=[send_scratch, pltpu.SemaphoreType.DMA((9,))],
        compiler_params=PARAMS,
        cost_estimate=pl.CostEstimate(flops=1 << 20, bytes_accessed=1 << 20, transcendentals=0),
    )(blocks, send_lists)
    plan, mask = pl.pallas_call(
        plan_kernel,
        out_shape=[
            jax.ShapeDtypeStruct((72,), jnp.int32),
            jax.ShapeDtypeStruct((8, SIDE), jnp.int32),
        ],
        in_specs=[HBM] * 4,
        out_specs=[SMEM, VMEM],
        scratch_shapes=[
            pltpu.SMEM((32,), jnp.int32),
            pltpu.SMEM((32,), jnp.int32),
            send_scratch,
            pltpu.SemaphoreType.DMA((4,)),
        ],
        compiler_params=PARAMS,
        cost_estimate=pl.CostEstimate(flops=1 << 20, bytes_accessed=1 << 20, transcendentals=0),
    )(tile_rows, tile_cols, send_lists, mask)
    anchor = None
    for iteration in range(ITERS):
        first = iteration == 0
        last = iteration == ITERS - 1
        wide = lax.ppermute(wide, dom, adjacent)
        narrow = lax.ppermute(narrow, dom, three_away)
        parts, relay = pl.pallas_call(
            mass_kernel,
            out_shape=[shape(16, 16, SIDE), shape(6, SIDE, SIDE)],
            in_specs=[SMEM] + [VMEM] * 4,
            out_specs=[VMEM, VMEM],
            scratch_shapes=[pltpu.VMEM((16, SIDE), F32)],
            compiler_params=PARAMS,
        )(plan, source, own, wide, narrow)
        relay = lax.ppermute(relay, "core", [(0, 1), (1, 0)])
        parts = lax.all_to_all(parts, ("core", "cls"), 0, 0)
        out_shape = [own_shape] * (2 if first else 1)
        out_shape += [shape(8, 8, SIDE)] if last else swap_shapes
        results = pl.pallas_call(
            lambda *refs, first=first, last=last: spread_kernel(first, last, *refs),
            out_shape=out_shape,
            in_specs=[VMEM, SMEM] + [VMEM] * 5,
            out_specs=[VMEM] * len(out_shape),
            scratch_shapes=[
                pltpu.VMEM((16, 2 * SIDE, SIDE), jnp.bfloat16),
                pltpu.VMEM((32, SIDE, SIDE), F32),
            ],
            compiler_params=PARAMS,
        )(tiles, plan, mask if first else anchor, source, wide, relay, parts)
        if first:
            anchor, *results = results
        if last:
            source, parts = results
        else:
            source, wide, narrow, own = results
    parts = lax.all_to_all(parts, "cls", 0, 0)
    out = pl.pallas_call(
        last_kernel,
        out_shape=own_shape,
        in_specs=[VMEM, VMEM],
        out_specs=HBM,
        scratch_shapes=[pltpu.VMEM((8, SIDE, SIDE), F32), pltpu.SemaphoreType.DMA((8,))],
        compiler_params=PARAMS,
    )(source, parts)
    return out.reshape(8 * SIDE, SIDE)


def solution(mesh):
    split_mesh = Mesh(
        mesh.devices.reshape(mesh.shape["dom"] // 2, 2, mesh.shape["cls"]), ("chip", "core", "cls")
    )
    dom = ("chip", "core")
    return jax.shard_map(
        on_device,
        mesh=split_mesh,
        in_specs=(P(dom, None, None), P(dom), P(dom), P(dom, None, None), P(dom), P(dom, "cls")),
        out_specs=P(dom, "cls"),
        check_vma=False,
    )
```

```python
import functools

import jax
import jax.numpy as jnp
from jax import lax
from jax.experimental import pallas as pl
from jax.experimental.pallas import tpu as pltpu
from jax.sharding import Mesh
from jax.sharding import PartitionSpec as P

CLASSES = 1024
ITERS = 3
SIDE = 128

VMEM = pl.BlockSpec(memory_space=pltpu.VMEM)
SMEM = pl.BlockSpec(memory_space=pltpu.SMEM)
HBM = pl.BlockSpec(memory_space=pltpu.HBM)
F32 = jnp.float32
PARAMS = pltpu.CompilerParams(vmem_limit_bytes=16 * 1024 * 1024)


def shape(*dims):
    return jax.ShapeDtypeStruct(dims, F32)


def shift_right(value, by):
    return lax.shift_right_logical(value, by)


def plan_entries(rows, cols, send):
    core = lax.axis_index("core")
    for tile in range(32):
        yield rows[tile]
    for tile in range(32):
        col = cols[tile]
        ghost = jnp.maximum(col - 8, 0)
        offset = shift_right(ghost, 1)
        half = shift_right(offset, 1)
        pair = jnp.where(lax.rem(offset, 2) == 1, 2 + (half ^ (1 - core)), half ^ core)
        yield jnp.where(col < 8, col, 8 + 2 * pair + lax.rem(ghost, 2))
    for offset in range(4):
        for within in range(2):
            yield send[0, within, offset]


def row_block(plan, tile):
    return plan[tile]


def operand_block(plan, tile):
    return plan[32 + tile]


def sent_block(plan, offset, within):
    return plan[64 + 2 * offset + within]


def block_at(ref, place):
    return ref[SIDE * place : SIDE * (place + 1), :]


def fill_swaps(source, sums, block_of, wide, narrow, near, rows):
    core = lax.axis_index("core")
    rows[0:8, :] = sums
    rows[8:16, :] = jnp.zeros((8, SIDE), F32)
    for within in range(2):
        block = block_of(2 * core, within)
        near[within] = source[block]
        rows[10 + within : 11 + within, :] = rows[pl.ds(block, 1), :]
    for out, offsets in ((wide, (2 - 2 * core, 3 - 2 * core)), (narrow, (1 + 2 * core,))):
        count = 2 * len(offsets)
        out[count * SIDE + count :, :] = jnp.zeros((8 - count, SIDE), F32)
        for part, offset in enumerate(offsets):
            for within in range(2):
                place = 2 * part + within
                block = block_of(offset, within)
                out[SIDE * place : SIDE * (place + 1), :] = source[block]
                out[count * SIDE + place : count * SIDE + place + 1, :] = rows[pl.ds(block, 1), :]


def lane_sums(block):
    return jnp.sum(jnp.transpose(block), axis=0, keepdims=True)


def copy_all(pairs, sems):
    copies = []
    for number, (here, there) in enumerate(pairs):
        copy = pltpu.make_async_copy(here, there, sems.at[number])
        copy.start()
        copies.append(copy)
    return copies


def first_kernel(labels, send, kept, wide, narrow, near, rows, send_here, sems):
    pairs = [(labels.at[block], kept.at[block]) for block in range(8)]
    copies = copy_all([(send, send_here)] + pairs, sems)
    sums = []
    for block in range(8):
        copies[1 + block].wait()
        sums.append(lane_sums(kept[block]))
    copies[0].wait()
    block_of = lambda offset, within: send_here[0, within, offset]
    fill_swaps(kept, jnp.concatenate(sums, axis=0), block_of, wide, narrow, near, rows)


def plan_kernel(rows, cols, send, mask, plan, mask_kept, rows_here, cols_here, send_here, sems):
    copies = copy_all([(rows, rows_here), (cols, cols_here), (send, send_here), (mask, mask_kept)], sems)
    for copy in copies:
        copy.wait()
    for place, entry in enumerate(plan_entries(rows_here, cols_here, send_here)):
        plan[place] = entry


def mass_kernel(sums, near, wide, narrow, plan, parts, relay, rows):
    rows[...] = sums[...]
    rows[8:10, :] = wide[4 * SIDE : 4 * SIDE + 2, :]
    rows[12:14, :] = wide[4 * SIDE + 2 : 4 * SIDE + 4, :]
    rows[14:16, :] = narrow[2 * SIDE : 2 * SIDE + 2, :]
    for within in range(2):
        relay[within] = near[within]
        relay[2 + within] = block_at(wide, 2 + within)
        relay[4 + within] = block_at(narrow, within)
    partial = rows[...]
    for share in range(16):
        parts[share] = partial


def scales(total, blocks):
    scale = CLASSES / total
    full = jnp.concatenate([scale, jnp.zeros((SIDE - blocks, SIDE), F32)], axis=0)
    return jnp.transpose(full)


def total_of(parts, core):
    total = parts[8 * core]
    for share in range(1, 8):
        total = total + parts[8 * core + share]
    return total


def split(value):
    high = value.astype(jnp.bfloat16)
    low = (value - high.astype(F32)).astype(jnp.bfloat16)
    return high, low


def spread_kernel(first, last, *refs):
    refs = list(refs)
    tiles, plan, mask, source, wide, relay, parts = refs[:7]
    refs = refs[7:]
    anchor = refs.pop(0) if first else mask
    squared = refs.pop(0)
    if last:
        own_parts, *refs = refs
    else:
        wide_out, narrow_out, near_out, rows_out, *refs = refs
    operand, products, plan_here, plan_sem = refs
    plan_copy = pltpu.make_async_copy(plan, plan_here, plan_sem)
    plan_copy.start()
    core = lax.axis_index("core")
    mine = total_of(parts, core)
    mate = total_of(parts, 1 - core)
    scale = scales(jnp.concatenate([mine[0:10], mate[10:16]], axis=0), 16)
    if first:
        seeded = jnp.concatenate(
            [mask[...].astype(F32), jnp.zeros((SIDE - 8, SIDE), F32)], axis=0
        )
        seeded = 64.0 * jnp.transpose(seeded)
    for block in range(16):
        if block < 8:
            value = source[block]
        elif block < 10:
            value = block_at(wide, block - 8)
        else:
            value = relay[block - 10]
        value = value * scale[:, block : block + 1]
        if first and block < 8:
            anchor[block] = seeded[:, block : block + 1] * value + 4.0
        high, low = split(value)
        operand[block, :SIDE, :] = high
        operand[block, SIDE:, :] = low
    plan_copy.wait()
    plan = plan_here
    for tile in range(32):
        weights = tiles[tile]
        products[tile] = jnp.dot(
            jnp.concatenate([weights, weights], axis=1),
            operand[operand_block(plan, tile)],
            preferred_element_type=F32,
        )
    squared[...] = anchor[...]
    for tile in range(32):
        row = row_block(plan, tile)
        squared[row] = squared[row] + products[tile]
    sums = []
    for block in range(8):
        value = squared[block]
        value = value * value
        squared[block] = value
        sums.append(lane_sums(value))
    sums = jnp.concatenate(sums, axis=0)
    if last:
        for share in range(8):
            own_parts[share] = sums
    else:
        block_of = functools.partial(sent_block, plan)
        fill_swaps(squared, sums, block_of, wide_out, narrow_out, near_out, rows_out)


def last_kernel(squared, parts, out, scaled, sems):
    scale = scales(total_of(parts, 0), 8)
    copies = []
    for block in range(8):
        scaled[block] = squared[block] * scale[:, block : block + 1]
        copy = pltpu.make_async_copy(scaled.at[block], out.at[block], sems.at[block])
        copy.start()
        copies.append(copy)
    for copy in copies:
        copy.wait()


def on_device(tiles, tile_rows, tile_cols, send_lists, seed_mask, labels):
    dom = ("chip", "core")
    count = 2 * lax.axis_size("chip")
    adjacent = [(i, (i + (1 if i % 2 else -1)) % count) for i in range(count)]
    three_away = [(i, (i + (-3 if i % 2 else 3)) % count) for i in range(count)]
    send_lists = jnp.transpose(send_lists, (0, 2, 1))
    own_shape = shape(8, SIDE, SIDE)
    sent_shapes = [
        shape(4 * SIDE + 8, SIDE),
        shape(2 * SIDE + 8, SIDE),
        shape(2, SIDE, SIDE),
        shape(16, SIDE),
    ]
    blocks, tile_rows, tile_cols, send_lists, mask = [
        pltpu.with_memory_space_constraint(value, pltpu.HBM)
        for value in (
            labels.reshape(8, SIDE, SIDE),
            tile_rows,
            tile_cols,
            send_lists,
            seed_mask.reshape(8, SIDE),
        )
    ]
    send_scratch = pltpu.SMEM((1, 2, 4), jnp.int32)
    source, wide, narrow, near, rows = pl.pallas_call(
        first_kernel,
        out_shape=[own_shape] + sent_shapes,
        in_specs=[HBM] * 2,
        out_specs=[VMEM] * 5,
        scratch_shapes=[send_scratch, pltpu.SemaphoreType.DMA((9,))],
        compiler_params=PARAMS,
        cost_estimate=pl.CostEstimate(flops=1 << 20, bytes_accessed=1 << 20, transcendentals=0),
    )(blocks, send_lists)
    plan, mask = pl.pallas_call(
        plan_kernel,
        out_shape=[
            jax.ShapeDtypeStruct((72,), jnp.int32),
            jax.ShapeDtypeStruct((8, SIDE), jnp.int32),
        ],
        in_specs=[HBM] * 4,
        out_specs=[SMEM, VMEM],
        scratch_shapes=[
            pltpu.SMEM((32,), jnp.int32),
            pltpu.SMEM((32,), jnp.int32),
            send_scratch,
            pltpu.SemaphoreType.DMA((4,)),
        ],
        compiler_params=PARAMS,
        cost_estimate=pl.CostEstimate(flops=1 << 20, bytes_accessed=1 << 20, transcendentals=0),
    )(tile_rows, tile_cols, send_lists, mask)
    anchor = None
    for iteration in range(ITERS):
        first = iteration == 0
        last = iteration == ITERS - 1
        wide = lax.ppermute(wide, dom, adjacent)
        narrow = lax.ppermute(narrow, dom, three_away)
        parts, relay = pl.pallas_call(
            mass_kernel,
            out_shape=[shape(16, 16, SIDE), shape(6, SIDE, SIDE)],
            in_specs=[VMEM] * 5,
            out_specs=[VMEM, VMEM],
            scratch_shapes=[pltpu.VMEM((16, SIDE), F32)],
            compiler_params=PARAMS,
        )(rows, near, wide, narrow, plan)
        relay = lax.ppermute(relay, "core", [(0, 1), (1, 0)])
        parts = lax.all_to_all(parts, ("core", "cls"), 0, 0)
        out_shape = [own_shape] * (2 if first else 1)
        out_shape += [shape(8, 8, SIDE)] if last else sent_shapes
        results = pl.pallas_call(
            lambda *refs, first=first, last=last: spread_kernel(first, last, *refs),
            out_shape=out_shape,
            in_specs=[VMEM] * 7,
            out_specs=[VMEM] * len(out_shape),
            scratch_shapes=[
                pltpu.VMEM((16, 2 * SIDE, SIDE), jnp.bfloat16),
                pltpu.VMEM((32, SIDE, SIDE), F32),
                pltpu.SMEM((72,), jnp.int32),
                pltpu.SemaphoreType.DMA,
            ],
            compiler_params=PARAMS,
        )(tiles, plan, mask if first else anchor, source, wide, relay, parts)
        if first:
            anchor, *results = results
        if last:
            source, parts = results
        else:
            source, wide, narrow, near, rows = results
    parts = lax.all_to_all(parts, "cls", 0, 0)
    out = pl.pallas_call(
        last_kernel,
        out_shape=own_shape,
        in_specs=[VMEM, VMEM],
        out_specs=HBM,
        scratch_shapes=[pltpu.VMEM((8, SIDE, SIDE), F32), pltpu.SemaphoreType.DMA((8,))],
        compiler_params=PARAMS,
    )(source, parts)
    return out.reshape(8 * SIDE, SIDE)


def solution(mesh):
    split_mesh = Mesh(
        mesh.devices.reshape(mesh.shape["dom"] // 2, 2, mesh.shape["cls"]), ("chip", "core", "cls")
    )
    dom = ("chip", "core")
    return jax.shard_map(
        on_device,
        mesh=split_mesh,
        in_specs=(P(dom, None, None), P(dom), P(dom), P(dom, None, None), P(dom), P(dom, "cls")),
        out_specs=P(dom, "cls"),
        check_vma=False,
    )
```

```python
import functools

import jax
import jax.numpy as jnp
from jax import lax
from jax.experimental import pallas as pl
from jax.experimental.pallas import tpu as pltpu
from jax.sharding import Mesh
from jax.sharding import PartitionSpec as P

CLASSES = 1024
ITERS = 3
SIDE = 128

VMEM = pl.BlockSpec(memory_space=pltpu.VMEM)
SMEM = pl.BlockSpec(memory_space=pltpu.SMEM)
HBM = pl.BlockSpec(memory_space=pltpu.HBM)
F32 = jnp.float32
PARAMS = pltpu.CompilerParams(vmem_limit_bytes=16 * 1024 * 1024)


def shape(*dims):
    return jax.ShapeDtypeStruct(dims, F32)


def shift_right(value, by):
    return lax.shift_right_logical(value, by)


def plan_entries(rows, cols, send):
    core = lax.axis_index("core")
    odd = lax.rem(lax.axis_index("chip"), 2)
    for tile in range(32):
        yield rows[tile]
    for tile in range(32):
        col = cols[tile]
        ghost = jnp.maximum(col - 8, 0)
        offset = shift_right(ghost, 1)
        half = shift_right(offset, 1)
        pair = jnp.where(lax.rem(offset, 2) == 1, 2 * (half ^ odd), 1 + 2 * (half ^ core))
        yield jnp.where(col < 8, col, 8 + 2 * pair + lax.rem(ghost, 2))
    for offset in range(4):
        for within in range(2):
            yield send[0, within, offset]


def row_block(plan, tile):
    return plan[tile]


def operand_block(plan, tile):
    return plan[32 + tile]


def sent_block(plan, offset, within):
    return plan[64 + 2 * offset + within]


def block_at(ref, place):
    return ref[SIDE * place : SIDE * (place + 1), :]


def fill_swaps(source, sums, block_of, outs, rows):
    core = lax.axis_index("core")
    odd = lax.rem(lax.axis_index("chip"), 2)
    rows[0:8, :] = sums
    for out, offset in zip(outs, (3 - 2 * odd, 2 - 2 * core, 1 + 2 * odd, 2 * core)):
        out[2 * SIDE + 2 :, :] = jnp.zeros((6, SIDE), F32)
        for within in range(2):
            block = block_of(offset, within)
            out[SIDE * within : SIDE * (within + 1), :] = source[block]
            out[2 * SIDE + within : 2 * SIDE + within + 1, :] = rows[pl.ds(block, 1), :]


def lane_sums(block):
    return jnp.sum(jnp.transpose(block), axis=0, keepdims=True)


def copy_all(pairs, sems):
    copies = []
    for number, (here, there) in enumerate(pairs):
        copy = pltpu.make_async_copy(here, there, sems.at[number])
        copy.start()
        copies.append(copy)
    return copies


def first_kernel(labels, send, kept, out0, out1, out2, out3, rows, send_here, sems):
    pairs = [(labels.at[block], kept.at[block]) for block in range(8)]
    copies = copy_all([(send, send_here)] + pairs, sems)
    sums = []
    for block in range(8):
        copies[1 + block].wait()
        sums.append(lane_sums(kept[block]))
    copies[0].wait()
    block_of = lambda offset, within: send_here[0, within, offset]
    fill_swaps(kept, jnp.concatenate(sums, axis=0), block_of, (out0, out1, out2, out3), rows)


def plan_kernel(rows, cols, send, mask, plan, mask_kept, rows_here, cols_here, send_here, sems):
    copies = copy_all([(rows, rows_here), (cols, cols_here), (send, send_here), (mask, mask_kept)], sems)
    for copy in copies:
        copy.wait()
    for place, entry in enumerate(plan_entries(rows_here, cols_here, send_here)):
        plan[place] = entry


def mass_kernel(sums, in0, in1, in2, in3, plan, parts):
    received = [ref[2 * SIDE : 2 * SIDE + 2, :] for ref in (in0, in1, in2, in3)]
    partial = jnp.concatenate([sums[...]] + received, axis=0)
    for share in range(8):
        parts[share] = partial


def scales(total, blocks):
    scale = CLASSES / total
    full = jnp.concatenate([scale, jnp.zeros((SIDE - blocks, SIDE), F32)], axis=0)
    return jnp.transpose(full)


def total_of(parts):
    total = parts[0]
    for share in range(1, 8):
        total = total + parts[share]
    return total


def split(value):
    high = value.astype(jnp.bfloat16)
    low = (value - high.astype(F32)).astype(jnp.bfloat16)
    return high, low


def spread_kernel(first, last, *refs):
    refs = list(refs)
    tiles, plan, mask, source = refs[:4]
    received = refs[4:8]
    parts = refs[8]
    refs = refs[9:]
    anchor = refs.pop(0) if first else mask
    squared = refs.pop(0)
    if last:
        own_parts, *refs = refs
    else:
        *outs, rows_out = refs[:5]
        refs = refs[5:]
    operand, products, plan_here, plan_sem = refs
    plan_copy = pltpu.make_async_copy(plan, plan_here, plan_sem)
    plan_copy.start()
    scale = scales(total_of(parts), 16)
    if first:
        seeded = jnp.concatenate(
            [mask[...].astype(F32), jnp.zeros((SIDE - 8, SIDE), F32)], axis=0
        )
        seeded = 64.0 * jnp.transpose(seeded)
    for block in range(16):
        if block < 8:
            value = source[block]
        else:
            value = block_at(received[(block - 8) // 2], block % 2)
        value = value * scale[:, block : block + 1]
        if first and block < 8:
            anchor[block] = seeded[:, block : block + 1] * value + 4.0
        high, low = split(value)
        operand[block, :SIDE, :] = high
        operand[block, SIDE:, :] = low
    plan_copy.wait()
    plan = plan_here
    for tile in range(32):
        weights = tiles[tile]
        products[tile] = jnp.dot(
            jnp.concatenate([weights, weights], axis=1),
            operand[operand_block(plan, tile)],
            preferred_element_type=F32,
        )
    squared[...] = anchor[...]
    for tile in range(32):
        row = row_block(plan, tile)
        squared[row] = squared[row] + products[tile]
    sums = []
    for block in range(8):
        value = squared[block]
        value = value * value
        squared[block] = value
        sums.append(lane_sums(value))
    sums = jnp.concatenate(sums, axis=0)
    if last:
        for share in range(8):
            own_parts[share] = sums
    else:
        block_of = functools.partial(sent_block, plan)
        fill_swaps(squared, sums, block_of, outs, rows_out)


def last_kernel(squared, parts, out, scaled, sems):
    scale = scales(total_of(parts), 8)
    copies = []
    for block in range(8):
        scaled[block] = squared[block] * scale[:, block : block + 1]
        copy = pltpu.make_async_copy(scaled.at[block], out.at[block], sems.at[block])
        copy.start()
        copies.append(copy)
    for copy in copies:
        copy.wait()


def on_device(tiles, tile_rows, tile_cols, send_lists, seed_mask, labels):
    dom = ("chip", "core")
    count = 2 * lax.axis_size("chip")
    swaps = [
        [(i, (i + (2 if i // 2 % 2 else -2)) % count) for i in range(count)],
        [(i, (i + (1 if i % 2 else -1)) % count) for i in range(count)],
        [(i, (i + (-2 if i // 2 % 2 else 2)) % count) for i in range(count)],
        [(i, i ^ 1) for i in range(count)],
    ]
    send_lists = jnp.transpose(send_lists, (0, 2, 1))
    own_shape = shape(8, SIDE, SIDE)
    sent_shapes = [shape(2 * SIDE + 8, SIDE)] * 4 + [shape(8, SIDE)]
    blocks, tile_rows, tile_cols, send_lists, mask = [
        pltpu.with_memory_space_constraint(value, pltpu.HBM)
        for value in (
            labels.reshape(8, SIDE, SIDE),
            tile_rows,
            tile_cols,
            send_lists,
            seed_mask.reshape(8, SIDE),
        )
    ]
    send_scratch = pltpu.SMEM((1, 2, 4), jnp.int32)
    source, *outs, rows = pl.pallas_call(
        first_kernel,
        out_shape=[own_shape] + sent_shapes,
        in_specs=[HBM] * 2,
        out_specs=[VMEM] * 6,
        scratch_shapes=[send_scratch, pltpu.SemaphoreType.DMA((9,))],
        compiler_params=PARAMS,
        cost_estimate=pl.CostEstimate(flops=1 << 20, bytes_accessed=1 << 20, transcendentals=0),
    )(blocks, send_lists)
    plan, mask = pl.pallas_call(
        plan_kernel,
        out_shape=[
            jax.ShapeDtypeStruct((72,), jnp.int32),
            jax.ShapeDtypeStruct((8, SIDE), jnp.int32),
        ],
        in_specs=[HBM] * 4,
        out_specs=[SMEM, VMEM],
        scratch_shapes=[
            pltpu.SMEM((32,), jnp.int32),
            pltpu.SMEM((32,), jnp.int32),
            send_scratch,
            pltpu.SemaphoreType.DMA((4,)),
        ],
        compiler_params=PARAMS,
        cost_estimate=pl.CostEstimate(flops=1 << 20, bytes_accessed=1 << 20, transcendentals=0),
    )(tile_rows, tile_cols, send_lists, mask)
    anchor = None
    for iteration in range(ITERS):
        first = iteration == 0
        last = iteration == ITERS - 1
        received = [lax.ppermute(out, dom, swap) for out, swap in zip(outs, swaps)]
        parts = pl.pallas_call(
            mass_kernel,
            out_shape=shape(8, 16, SIDE),
            in_specs=[VMEM] * 6,
            out_specs=VMEM,
            compiler_params=PARAMS,
        )(rows, *received, plan)
        parts = lax.all_to_all(parts, "cls", 0, 0)
        out_shape = [own_shape] * (2 if first else 1)
        out_shape += [shape(8, 8, SIDE)] if last else sent_shapes
        results = pl.pallas_call(
            lambda *refs, first=first, last=last: spread_kernel(first, last, *refs),
            out_shape=out_shape,
            in_specs=[VMEM] * 9,
            out_specs=[VMEM] * len(out_shape),
            scratch_shapes=[
                pltpu.VMEM((16, 2 * SIDE, SIDE), jnp.bfloat16),
                pltpu.VMEM((32, SIDE, SIDE), F32),
                pltpu.SMEM((72,), jnp.int32),
                pltpu.SemaphoreType.DMA,
            ],
            compiler_params=PARAMS,
        )(tiles, plan, mask if first else anchor, source, *received, parts)
        if first:
            anchor, *results = results
        if last:
            source, parts = results
        else:
            source, *outs, rows = results
    parts = lax.all_to_all(parts, "cls", 0, 0)
    out = pl.pallas_call(
        last_kernel,
        out_shape=own_shape,
        in_specs=[VMEM, VMEM],
        out_specs=HBM,
        scratch_shapes=[pltpu.VMEM((8, SIDE, SIDE), F32), pltpu.SemaphoreType.DMA((8,))],
        compiler_params=PARAMS,
    )(source, parts)
    return out.reshape(8 * SIDE, SIDE)


def solution(mesh):
    split_mesh = Mesh(
        mesh.devices.reshape(mesh.shape["dom"] // 2, 2, mesh.shape["cls"]), ("chip", "core", "cls")
    )
    dom = ("chip", "core")
    return jax.shard_map(
        on_device,
        mesh=split_mesh,
        in_specs=(P(dom, None, None), P(dom), P(dom), P(dom, None, None), P(dom), P(dom, "cls")),
        out_specs=P(dom, "cls"),
        check_vma=False,
    )
```

```python
import jax
import jax.numpy as jnp
from jax import lax
from jax.experimental import pallas as pl
from jax.experimental.pallas import tpu as pltpu
from jax.sharding import Mesh
from jax.sharding import PartitionSpec as P

CLASSES = 1024
ITERS = 3
SIDE = 128

VMEM = pl.BlockSpec(memory_space=pltpu.VMEM)
SMEM = pl.BlockSpec(memory_space=pltpu.SMEM)
HBM = pl.BlockSpec(memory_space=pltpu.HBM)
F32 = jnp.float32
PARAMS = pltpu.CompilerParams(vmem_limit_bytes=16 * 1024 * 1024)


def shape(*dims):
    return jax.ShapeDtypeStruct(dims, F32)


def shift_right(value, by):
    return lax.shift_right_logical(value, by)


def operand_block(col):
    odd = lax.rem(lax.axis_index("chip"), 2)
    core = lax.axis_index("core")
    ghost = jnp.maximum(col - 8, 0)
    offset = shift_right(ghost, 1)
    half = shift_right(offset, 1)
    pair = jnp.where(lax.rem(offset, 2) == 1, half ^ odd, 2 + (half ^ core))
    return jnp.where(col < 8, col, 8 + 2 * pair + lax.rem(ghost, 2))


def block_at(ref, place):
    return ref[SIDE * place : SIDE * (place + 1), :]


def fill_swaps(source, sums, send, outs, rows):
    core = lax.axis_index("core")
    odd = lax.rem(lax.axis_index("chip"), 2)
    rows[0:8, :] = sums
    for out, offset in zip(outs, (3 - 2 * odd, 1 + 2 * odd, 2 - 2 * core, 2 * core)):
        out[2 * SIDE + 2 :, :] = jnp.zeros((6, SIDE), F32)
        for within in range(2):
            block = send[0, within, offset]
            out[SIDE * within : SIDE * (within + 1), :] = source[block]
            out[2 * SIDE + within : 2 * SIDE + within + 1, :] = rows[pl.ds(block, 1), :]


def lane_sums(block):
    return jnp.sum(jnp.transpose(block), axis=0, keepdims=True)


def copy_all(pairs, sems):
    copies = []
    for number, (here, there) in enumerate(pairs):
        copy = pltpu.make_async_copy(here, there, sems.at[number])
        copy.start()
        copies.append(copy)
    return copies


def first_kernel(labels, send, rows, cols, mask, kept, send_kept, rows_kept, cols_kept, mask_kept, *refs):
    *outs, sums_out, send_here, sems = refs
    pairs = [(send, send_here)]
    pairs += [(labels.at[block], kept.at[block]) for block in range(8)]
    pairs += [(send, send_kept), (rows, rows_kept), (cols, cols_kept), (mask, mask_kept)]
    copies = copy_all(pairs, sems)
    sums = []
    for block in range(8):
        copies[1 + block].wait()
        sums.append(lane_sums(kept[block]))
    copies[0].wait()
    fill_swaps(kept, jnp.concatenate(sums, axis=0), send_here, outs, sums_out)
    for copy in copies[9:]:
        copy.wait()


def mass_kernel(sums, in0, in1, in2, in3, parts):
    received = [ref[2 * SIDE : 2 * SIDE + 2, :] for ref in (in0, in1, in2, in3)]
    partial = jnp.concatenate([sums[...]] + received, axis=0)
    for share in range(8):
        parts[share] = partial


def scales(total, blocks):
    scale = CLASSES / total
    full = jnp.concatenate([scale, jnp.zeros((SIDE - blocks, SIDE), F32)], axis=0)
    return jnp.transpose(full)


def total_of(parts):
    total = parts[0]
    for share in range(1, 8):
        total = total + parts[share]
    return total


def split(value):
    high = value.astype(jnp.bfloat16)
    low = (value - high.astype(F32)).astype(jnp.bfloat16)
    return high, low


def spread_kernel(first, last, *refs):
    refs = list(refs)
    tiles, *indices = refs[:4]
    mask, source, *received = refs[4:10]
    parts = refs[10]
    refs = refs[11:]
    anchor = refs.pop(0) if first else mask
    squared = refs.pop(0)
    if last:
        own_parts, *refs = refs
    else:
        *outs, rows_out = refs[:5]
        refs = refs[5:]
    operand, products, send, rows, cols, sems = refs
    copies = copy_all(list(zip(indices, (send, rows, cols))), sems)
    scale = scales(total_of(parts), 16)
    if first:
        seeded = jnp.concatenate(
            [mask[...].astype(F32), jnp.zeros((SIDE - 8, SIDE), F32)], axis=0
        )
        seeded = 64.0 * jnp.transpose(seeded)
    for block in range(16):
        if block < 8:
            value = source[block]
        else:
            value = block_at(received[(block - 8) // 2], block % 2)
        value = value * scale[:, block : block + 1]
        if first and block < 8:
            anchor[block] = seeded[:, block : block + 1] * value + 4.0
        high, low = split(value)
        operand[block, :SIDE, :] = high
        operand[block, SIDE:, :] = low
    for copy in copies:
        copy.wait()
    for tile in range(32):
        weights = tiles[tile]
        products[tile] = jnp.dot(
            jnp.concatenate([weights, weights], axis=1),
            operand[operand_block(cols[tile])],
            preferred_element_type=F32,
        )
    squared[...] = anchor[...]
    for tile in range(32):
        row = rows[tile]
        squared[row] = squared[row] + products[tile]
    sums = []
    for block in range(8):
        value = squared[block]
        value = value * value
        squared[block] = value
        sums.append(lane_sums(value))
    sums = jnp.concatenate(sums, axis=0)
    if last:
        for share in range(8):
            own_parts[share] = sums
    else:
        fill_swaps(squared, sums, send, outs, rows_out)


def last_kernel(squared, parts, out, scaled, sems):
    scale = scales(total_of(parts), 8)
    copies = []
    for block in range(8):
        scaled[block] = squared[block] * scale[:, block : block + 1]
        copy = pltpu.make_async_copy(scaled.at[block], out.at[block], sems.at[block])
        copy.start()
        copies.append(copy)
    for copy in copies:
        copy.wait()


def on_device(tiles, tile_rows, tile_cols, send_lists, seed_mask, labels):
    dom = ("chip", "core")
    count = 2 * lax.axis_size("chip")
    swaps = [
        [(i, (i + (2 if i // 2 % 2 else -2)) % count) for i in range(count)],
        [(i, (i + (-2 if i // 2 % 2 else 2)) % count) for i in range(count)],
        [(i, (i + (1 if i % 2 else -1)) % count) for i in range(count)],
        [(i, i ^ 1) for i in range(count)],
    ]
    send_lists = jnp.transpose(send_lists, (0, 2, 1))
    own_shape = shape(8, SIDE, SIDE)
    sent_shapes = [shape(2 * SIDE + 8, SIDE)] * 4 + [shape(8, SIDE)]
    blocks, tile_rows, tile_cols, send_lists, mask = [
        pltpu.with_memory_space_constraint(value, pltpu.HBM)
        for value in (
            labels.reshape(8, SIDE, SIDE),
            tile_rows,
            tile_cols,
            send_lists,
            seed_mask.reshape(8, SIDE),
        )
    ]
    index_shapes = [(1, 2, 4), (32,), (32,)]
    index_scratch = [pltpu.SMEM(dims, jnp.int32) for dims in index_shapes]
    source, send_lists, tile_rows, tile_cols, mask, *outs, rows = pl.pallas_call(
        first_kernel,
        out_shape=[own_shape]
        + [jax.ShapeDtypeStruct(dims, jnp.int32) for dims in index_shapes + [(8, SIDE)]]
        + sent_shapes,
        in_specs=[HBM] * 5,
        out_specs=[VMEM] * 10,
        scratch_shapes=index_scratch[:1] + [pltpu.SemaphoreType.DMA((13,))],
        compiler_params=PARAMS,
        cost_estimate=pl.CostEstimate(flops=1 << 20, bytes_accessed=1 << 20, transcendentals=0),
    )(blocks, send_lists, tile_rows, tile_cols, mask)
    anchor = None
    for iteration in range(ITERS):
        first = iteration == 0
        last = iteration == ITERS - 1
        received = [lax.ppermute(out, dom, swap) for out, swap in zip(outs, swaps)]
        parts = pl.pallas_call(
            mass_kernel,
            out_shape=shape(8, 16, SIDE),
            in_specs=[VMEM] * 5,
            out_specs=VMEM,
            compiler_params=PARAMS,
        )(rows, *received)
        parts = lax.all_to_all(parts, "cls", 0, 0)
        out_shape = [own_shape] * (2 if first else 1)
        out_shape += [shape(8, 8, SIDE)] if last else sent_shapes
        results = pl.pallas_call(
            lambda *refs, first=first, last=last: spread_kernel(first, last, *refs),
            out_shape=out_shape,
            in_specs=[VMEM] * 11,
            out_specs=[VMEM] * len(out_shape),
            scratch_shapes=[
                pltpu.VMEM((16, 2 * SIDE, SIDE), jnp.bfloat16),
                pltpu.VMEM((32, SIDE, SIDE), F32),
            ]
            + index_scratch
            + [pltpu.SemaphoreType.DMA((3,))],
            compiler_params=PARAMS,
        )(
            tiles, send_lists, tile_rows, tile_cols, mask if first else anchor, source,
            *received, parts,
        )
        if first:
            anchor, *results = results
        if last:
            source, parts = results
        else:
            source, *outs, rows = results
    parts = lax.all_to_all(parts, "cls", 0, 0)
    out = pl.pallas_call(
        last_kernel,
        out_shape=own_shape,
        in_specs=[VMEM, VMEM],
        out_specs=HBM,
        scratch_shapes=[pltpu.VMEM((8, SIDE, SIDE), F32), pltpu.SemaphoreType.DMA((8,))],
        compiler_params=PARAMS,
    )(source, parts)
    return out.reshape(8 * SIDE, SIDE)


def solution(mesh):
    split_mesh = Mesh(
        mesh.devices.reshape(mesh.shape["dom"] // 2, 2, mesh.shape["cls"]), ("chip", "core", "cls")
    )
    dom = ("chip", "core")
    return jax.shard_map(
        on_device,
        mesh=split_mesh,
        in_specs=(P(dom, None, None), P(dom), P(dom), P(dom, None, None), P(dom), P(dom, "cls")),
        out_specs=P(dom, "cls"),
        check_vma=False,
    )
```

```python
import functools

import jax
import jax.numpy as jnp
from jax import lax
from jax.experimental import pallas as pl
from jax.experimental.pallas import tpu as pltpu
from jax.sharding import Mesh
from jax.sharding import PartitionSpec as P

CLASSES = 1024
ITERS = 3
SIDE = 128

VMEM = pl.BlockSpec(memory_space=pltpu.VMEM)
SMEM = pl.BlockSpec(memory_space=pltpu.SMEM)
HBM = pl.BlockSpec(memory_space=pltpu.HBM)
F32 = jnp.float32
PARAMS = pltpu.CompilerParams(vmem_limit_bytes=16 * 1024 * 1024)


def shape(*dims):
    return jax.ShapeDtypeStruct(dims, F32)


def shift_right(value, by):
    return lax.shift_right_logical(value, by)


def plan_entries(rows, cols, send):
    core = lax.axis_index("core")
    odd = lax.rem(lax.axis_index("chip"), 2)
    for tile in range(32):
        yield rows[tile]
    for tile in range(32):
        col = cols[tile]
        ghost = jnp.maximum(col - 8, 0)
        offset = shift_right(ghost, 1)
        half = shift_right(offset, 1)
        pair = jnp.where(lax.rem(offset, 2) == 1, 2 * (half ^ odd), 1 + 2 * (half ^ core))
        yield jnp.where(col < 8, col, 8 + 2 * pair + lax.rem(ghost, 2))
    for offset in range(4):
        for within in range(2):
            yield send[0, within, offset]


def row_block(plan, tile):
    return plan[tile]


def operand_block(plan, tile):
    return plan[32 + tile]


def sent_block(plan, offset, within):
    return plan[64 + 2 * offset + within]


def block_at(ref, place):
    return ref[SIDE * place : SIDE * (place + 1), :]


def fill_swaps(source, sums, block_of, outs, rows):
    core = lax.axis_index("core")
    odd = lax.rem(lax.axis_index("chip"), 2)
    rows[0:8, :] = sums
    for out, offset in zip(outs, (3 - 2 * odd, 2 - 2 * core, 1 + 2 * odd, 2 * core)):
        out[2 * SIDE + 2 :, :] = jnp.zeros((6, SIDE), F32)
        for within in range(2):
            block = block_of(offset, within)
            out[SIDE * within : SIDE * (within + 1), :] = source[block]
            out[2 * SIDE + within : 2 * SIDE + within + 1, :] = rows[pl.ds(block, 1), :]


def lane_sums(block):
    return jnp.sum(jnp.transpose(block), axis=0, keepdims=True)


def copy_all(pairs, sems):
    copies = []
    for number, (here, there) in enumerate(pairs):
        copy = pltpu.make_async_copy(here, there, sems.at[number])
        copy.start()
        copies.append(copy)
    return copies


def first_kernel(labels, send, rows, cols, mask, kept, plan, mask_kept, *refs):
    *outs, sums_out, send_here, rows_here, cols_here, plan_here, sems = refs
    pairs = [(send, send_here), (rows, rows_here), (cols, cols_here)]
    pairs += [(labels.at[block], kept.at[block]) for block in range(8)]
    copies = copy_all(pairs + [(mask, mask_kept)], sems)
    for copy in copies[:3]:
        copy.wait()
    for place, entry in enumerate(plan_entries(rows_here, cols_here, send_here)):
        plan_here[place] = entry
    plan_copy = pltpu.make_async_copy(plan_here, plan, sems.at[12])
    plan_copy.start()
    sums = []
    for block in range(8):
        copies[3 + block].wait()
        sums.append(lane_sums(kept[block]))
    block_of = lambda offset, within: send_here[0, within, offset]
    fill_swaps(kept, jnp.concatenate(sums, axis=0), block_of, outs, sums_out)
    copies[11].wait()
    plan_copy.wait()


def mass_kernel(sums, in0, in1, in2, in3, parts):
    received = [ref[2 * SIDE : 2 * SIDE + 2, :] for ref in (in0, in1, in2, in3)]
    partial = jnp.concatenate([sums[...]] + received, axis=0)
    for share in range(8):
        parts[share] = partial


def scales(total, blocks):
    scale = CLASSES / total
    full = jnp.concatenate([scale, jnp.zeros((SIDE - blocks, SIDE), F32)], axis=0)
    return jnp.transpose(full)


def total_of(parts):
    total = parts[0]
    for share in range(1, 8):
        total = total + parts[share]
    return total


def split(value):
    high = value.astype(jnp.bfloat16)
    low = (value - high.astype(F32)).astype(jnp.bfloat16)
    return high, low


def spread_kernel(first, last, *refs):
    refs = list(refs)
    tiles, plan, mask, source = refs[:4]
    received = refs[4:8]
    parts = refs[8]
    refs = refs[9:]
    anchor = refs.pop(0) if first else mask
    squared = refs.pop(0)
    if last:
        own_parts, *refs = refs
    else:
        *outs, rows_out = refs[:5]
        refs = refs[5:]
    operand, products, plan_here, plan_sem = refs
    plan_copy = pltpu.make_async_copy(plan, plan_here, plan_sem)
    plan_copy.start()
    scale = scales(total_of(parts), 16)
    if first:
        seeded = jnp.concatenate(
            [mask[...].astype(F32), jnp.zeros((SIDE - 8, SIDE), F32)], axis=0
        )
        seeded = 64.0 * jnp.transpose(seeded)
    for block in range(16):
        if block < 8:
            value = source[block]
        else:
            value = block_at(received[(block - 8) // 2], block % 2)
        value = value * scale[:, block : block + 1]
        if first and block < 8:
            anchor[block] = seeded[:, block : block + 1] * value + 4.0
        high, low = split(value)
        operand[block, :SIDE, :] = high
        operand[block, SIDE:, :] = low
    plan_copy.wait()
    plan = plan_here
    for tile in range(32):
        weights = tiles[tile]
        products[tile] = jnp.dot(
            jnp.concatenate([weights, weights], axis=1),
            operand[operand_block(plan, tile)],
            preferred_element_type=F32,
        )
    squared[...] = anchor[...]
    for tile in range(32):
        row = row_block(plan, tile)
        squared[row] = squared[row] + products[tile]
    sums = []
    for block in range(8):
        value = squared[block]
        value = value * value
        squared[block] = value
        sums.append(lane_sums(value))
    sums = jnp.concatenate(sums, axis=0)
    if last:
        for share in range(8):
            own_parts[share] = sums
    else:
        block_of = functools.partial(sent_block, plan)
        fill_swaps(squared, sums, block_of, outs, rows_out)


def last_kernel(squared, parts, out, scaled, sems):
    scale = scales(total_of(parts), 8)
    copies = []
    for block in range(8):
        scaled[block] = squared[block] * scale[:, block : block + 1]
        copy = pltpu.make_async_copy(scaled.at[block], out.at[block], sems.at[block])
        copy.start()
        copies.append(copy)
    for copy in copies:
        copy.wait()


def on_device(tiles, tile_rows, tile_cols, send_lists, seed_mask, labels):
    dom = ("chip", "core")
    count = 2 * lax.axis_size("chip")
    swaps = [
        [(i, (i + (2 if i // 2 % 2 else -2)) % count) for i in range(count)],
        [(i, (i + (1 if i % 2 else -1)) % count) for i in range(count)],
        [(i, (i + (-2 if i // 2 % 2 else 2)) % count) for i in range(count)],
        [(i, i ^ 1) for i in range(count)],
    ]
    send_lists = jnp.transpose(send_lists, (0, 2, 1))
    own_shape = shape(8, SIDE, SIDE)
    sent_shapes = [shape(2 * SIDE + 8, SIDE)] * 4 + [shape(8, SIDE)]
    blocks, tile_rows, tile_cols, send_lists, mask = [
        pltpu.with_memory_space_constraint(value, pltpu.HBM)
        for value in (
            labels.reshape(8, SIDE, SIDE),
            tile_rows,
            tile_cols,
            send_lists,
            seed_mask.reshape(8, SIDE),
        )
    ]
    plan_shape = jax.ShapeDtypeStruct((72,), jnp.int32)
    source, plan, mask, *outs, rows = pl.pallas_call(
        first_kernel,
        out_shape=[own_shape, plan_shape, jax.ShapeDtypeStruct((8, SIDE), jnp.int32)] + sent_shapes,
        in_specs=[HBM] * 5,
        out_specs=[VMEM] * 8,
        scratch_shapes=[
            pltpu.SMEM((1, 2, 4), jnp.int32),
            pltpu.SMEM((32,), jnp.int32),
            pltpu.SMEM((32,), jnp.int32),
            pltpu.SMEM((72,), jnp.int32),
            pltpu.SemaphoreType.DMA((13,)),
        ],
        compiler_params=PARAMS,
        cost_estimate=pl.CostEstimate(flops=1 << 20, bytes_accessed=1 << 20, transcendentals=0),
    )(blocks, send_lists, tile_rows, tile_cols, mask)
    anchor = None
    for iteration in range(ITERS):
        first = iteration == 0
        last = iteration == ITERS - 1
        received = [lax.ppermute(out, dom, swap) for out, swap in zip(outs, swaps)]
        parts = pl.pallas_call(
            mass_kernel,
            out_shape=shape(8, 16, SIDE),
            in_specs=[VMEM] * 5,
            out_specs=VMEM,
            compiler_params=PARAMS,
        )(rows, *received)
        parts = lax.all_to_all(parts, "cls", 0, 0)
        out_shape = [own_shape] * (2 if first else 1)
        out_shape += [shape(8, 8, SIDE)] if last else sent_shapes
        results = pl.pallas_call(
            lambda *refs, first=first, last=last: spread_kernel(first, last, *refs),
            out_shape=out_shape,
            in_specs=[VMEM] * 9,
            out_specs=[VMEM] * len(out_shape),
            scratch_shapes=[
                pltpu.VMEM((16, 2 * SIDE, SIDE), jnp.bfloat16),
                pltpu.VMEM((32, SIDE, SIDE), F32),
                pltpu.SMEM((72,), jnp.int32),
                pltpu.SemaphoreType.DMA,
            ],
            compiler_params=PARAMS,
        )(tiles, plan, mask if first else anchor, source, *received, parts)
        if first:
            anchor, *results = results
        if last:
            source, parts = results
        else:
            source, *outs, rows = results
    parts = lax.all_to_all(parts, "cls", 0, 0)
    out = pl.pallas_call(
        last_kernel,
        out_shape=own_shape,
        in_specs=[VMEM, VMEM],
        out_specs=HBM,
        scratch_shapes=[pltpu.VMEM((8, SIDE, SIDE), F32), pltpu.SemaphoreType.DMA((8,))],
        compiler_params=PARAMS,
    )(source, parts)
    return out.reshape(8 * SIDE, SIDE)


def solution(mesh):
    split_mesh = Mesh(
        mesh.devices.reshape(mesh.shape["dom"] // 2, 2, mesh.shape["cls"]), ("chip", "core", "cls")
    )
    dom = ("chip", "core")
    return jax.shard_map(
        on_device,
        mesh=split_mesh,
        in_specs=(P(dom, None, None), P(dom), P(dom), P(dom, None, None), P(dom), P(dom, "cls")),
        out_specs=P(dom, "cls"),
        check_vma=False,
    )
```

```python
import functools

import jax
import jax.numpy as jnp
from jax import lax
from jax.experimental import pallas as pl
from jax.experimental.pallas import tpu as pltpu
from jax.sharding import Mesh
from jax.sharding import PartitionSpec as P

CLASSES = 1024
ITERS = 3
SIDE = 128

VMEM = pl.BlockSpec(memory_space=pltpu.VMEM)
SMEM = pl.BlockSpec(memory_space=pltpu.SMEM)
HBM = pl.BlockSpec(memory_space=pltpu.HBM)
F32 = jnp.float32
PARAMS = pltpu.CompilerParams(vmem_limit_bytes=16 * 1024 * 1024)


def shape(*dims):
    return jax.ShapeDtypeStruct(dims, F32)


def shift_right(value, by):
    return lax.shift_right_logical(value, by)


def plan_entries(rows, cols, send):
    core = lax.axis_index("core")
    odd = lax.rem(lax.axis_index("chip"), 2)
    for tile in range(32):
        yield rows[tile]
    for tile in range(32):
        col = cols[tile]
        ghost = jnp.maximum(col - 8, 0)
        offset = shift_right(ghost, 1)
        half = shift_right(offset, 1)
        pair = jnp.where(lax.rem(offset, 2) == 1, 2 * (half ^ odd), 1 + 2 * (half ^ core))
        yield jnp.where(col < 8, col, 8 + 2 * pair + lax.rem(ghost, 2))
    for offset in range(4):
        for within in range(2):
            yield send[0, within, offset]


def row_block(plan, tile):
    return plan[tile]


def operand_block(plan, tile):
    return plan[32 + tile]


def sent_block(plan, offset, within):
    return plan[64 + 2 * offset + within]


def block_at(ref, place):
    return ref[SIDE * place : SIDE * (place + 1), :]


def fill_swaps(source, sums, block_of, outs, rows):
    core = lax.axis_index("core")
    odd = lax.rem(lax.axis_index("chip"), 2)
    rows[0:8, :] = sums
    for out, offset in zip(outs, (3 - 2 * odd, 2 - 2 * core, 1 + 2 * odd, 2 * core)):
        out[2 * SIDE + 2 :, :] = jnp.zeros((6, SIDE), F32)
        for within in range(2):
            block = block_of(offset, within)
            out[SIDE * within : SIDE * (within + 1), :] = source[block]
            out[2 * SIDE + within : 2 * SIDE + within + 1, :] = rows[pl.ds(block, 1), :]


def class_sums(block):
    return jnp.sum(block, axis=0, keepdims=True)


def copy_all(pairs, sems):
    copies = []
    for number, (here, there) in enumerate(pairs):
        copy = pltpu.make_async_copy(here, there, sems.at[number])
        copy.start()
        copies.append(copy)
    return copies


def first_kernel(labels, send, rows, cols, mask, kept, plan, mask_kept, *refs):
    *outs, sums_out, fetched, send_here, rows_here, cols_here, plan_here, sems = refs
    pairs = [(send, send_here), (rows, rows_here), (cols, cols_here)]
    pairs += [(labels.at[block], fetched.at[block]) for block in range(8)]
    copies = copy_all(pairs + [(mask, mask_kept)], sems)
    for copy in copies[:3]:
        copy.wait()
    for place, entry in enumerate(plan_entries(rows_here, cols_here, send_here)):
        plan_here[place] = entry
    plan_copy = pltpu.make_async_copy(plan_here, plan, sems.at[12])
    plan_copy.start()
    sums = []
    for block in range(8):
        copies[3 + block].wait()
        value = jnp.transpose(fetched[block])
        kept[block] = value
        sums.append(class_sums(value))
    block_of = lambda offset, within: send_here[0, within, offset]
    fill_swaps(kept, jnp.concatenate(sums, axis=0), block_of, outs, sums_out)
    copies[11].wait()
    plan_copy.wait()


def mass_kernel(sums, in0, in1, in2, in3, parts):
    received = [ref[2 * SIDE : 2 * SIDE + 2, :] for ref in (in0, in1, in2, in3)]
    partial = jnp.concatenate([sums[...]] + received, axis=0)
    for share in range(8):
        parts[share] = partial


def total_of(parts):
    total = parts[0]
    for share in range(1, 8):
        total = total + parts[share]
    return total


def split(value):
    high = value.astype(jnp.bfloat16)
    low = (value - high.astype(F32)).astype(jnp.bfloat16)
    return high, low


def spread_kernel(first, last, *refs):
    refs = list(refs)
    tiles, plan, mask, source = refs[:4]
    received = refs[4:8]
    parts = refs[8]
    refs = refs[9:]
    anchor = refs.pop(0) if first else mask
    squared = refs.pop(0)
    if last:
        own_parts, *refs = refs
    else:
        *outs, rows_out = refs[:5]
        refs = refs[5:]
    operand, products, plan_here, plan_sem = refs
    plan_copy = pltpu.make_async_copy(plan, plan_here, plan_sem)
    plan_copy.start()
    scale = CLASSES / total_of(parts)
    if first:
        seeded = 64.0 * mask[...].astype(F32)
    for block in range(16):
        if block < 8:
            value = source[block]
        else:
            value = block_at(received[(block - 8) // 2], block % 2)
        value = value * scale[block : block + 1, :]
        if first and block < 8:
            anchor[block] = seeded[block : block + 1, :] * value + 4.0
        high, low = split(value)
        operand[block, :SIDE, :] = high
        operand[block, SIDE:, :] = low
    plan_copy.wait()
    plan = plan_here
    for tile in range(32):
        halves = lax.dot_general(
            operand[operand_block(plan, tile)],
            tiles[tile],
            (((1,), (1,)), ((), ())),
            preferred_element_type=F32,
        )
        products[tile] = halves[:SIDE] + halves[SIDE:]
    squared[...] = anchor[...]
    for tile in range(32):
        row = row_block(plan, tile)
        squared[row] = squared[row] + products[tile]
    sums = []
    for block in range(8):
        value = squared[block]
        value = value * value
        squared[block] = value
        sums.append(class_sums(value))
    sums = jnp.concatenate(sums, axis=0)
    if last:
        for share in range(8):
            own_parts[share] = sums
    else:
        block_of = functools.partial(sent_block, plan)
        fill_swaps(squared, sums, block_of, outs, rows_out)


def last_kernel(squared, parts, out, scaled, sems):
    scale = CLASSES / total_of(parts)
    copies = []
    for block in range(8):
        scaled[block] = jnp.transpose(squared[block] * scale[block : block + 1, :])
        copy = pltpu.make_async_copy(scaled.at[block], out.at[block], sems.at[block])
        copy.start()
        copies.append(copy)
    for copy in copies:
        copy.wait()


def on_device(tiles, tile_rows, tile_cols, send_lists, seed_mask, labels):
    dom = ("chip", "core")
    count = 2 * lax.axis_size("chip")
    swaps = [
        [(i, (i + (2 if i // 2 % 2 else -2)) % count) for i in range(count)],
        [(i, (i + (1 if i % 2 else -1)) % count) for i in range(count)],
        [(i, (i + (-2 if i // 2 % 2 else 2)) % count) for i in range(count)],
        [(i, i ^ 1) for i in range(count)],
    ]
    send_lists = jnp.transpose(send_lists, (0, 2, 1))
    own_shape = shape(8, SIDE, SIDE)
    sent_shapes = [shape(2 * SIDE + 8, SIDE)] * 4 + [shape(8, SIDE)]
    blocks, tile_rows, tile_cols, send_lists, mask = [
        pltpu.with_memory_space_constraint(value, pltpu.HBM)
        for value in (
            labels.reshape(8, SIDE, SIDE),
            tile_rows,
            tile_cols,
            send_lists,
            seed_mask.reshape(8, SIDE),
        )
    ]
    plan_shape = jax.ShapeDtypeStruct((72,), jnp.int32)
    source, plan, mask, *outs, rows = pl.pallas_call(
        first_kernel,
        out_shape=[own_shape, plan_shape, jax.ShapeDtypeStruct((8, SIDE), jnp.int32)] + sent_shapes,
        in_specs=[HBM] * 5,
        out_specs=[VMEM] * 8,
        scratch_shapes=[
            pltpu.VMEM((8, SIDE, SIDE), F32),
            pltpu.SMEM((1, 2, 4), jnp.int32),
            pltpu.SMEM((32,), jnp.int32),
            pltpu.SMEM((32,), jnp.int32),
            pltpu.SMEM((72,), jnp.int32),
            pltpu.SemaphoreType.DMA((13,)),
        ],
        compiler_params=PARAMS,
        cost_estimate=pl.CostEstimate(flops=1 << 20, bytes_accessed=1 << 20, transcendentals=0),
    )(blocks, send_lists, tile_rows, tile_cols, mask)
    anchor = None
    for iteration in range(ITERS):
        first = iteration == 0
        last = iteration == ITERS - 1
        received = [lax.ppermute(out, dom, swap) for out, swap in zip(outs, swaps)]
        parts = pl.pallas_call(
            mass_kernel,
            out_shape=shape(8, 16, SIDE),
            in_specs=[VMEM] * 5,
            out_specs=VMEM,
            compiler_params=PARAMS,
        )(rows, *received)
        parts = lax.all_to_all(parts, "cls", 0, 0)
        out_shape = [own_shape] * (2 if first else 1)
        out_shape += [shape(8, 8, SIDE)] if last else sent_shapes
        results = pl.pallas_call(
            lambda *refs, first=first, last=last: spread_kernel(first, last, *refs),
            out_shape=out_shape,
            in_specs=[VMEM] * 9,
            out_specs=[VMEM] * len(out_shape),
            scratch_shapes=[
                pltpu.VMEM((16, 2 * SIDE, SIDE), jnp.bfloat16),
                pltpu.VMEM((32, SIDE, SIDE), F32),
                pltpu.SMEM((72,), jnp.int32),
                pltpu.SemaphoreType.DMA,
            ],
            compiler_params=PARAMS,
        )(tiles, plan, mask if first else anchor, source, *received, parts)
        if first:
            anchor, *results = results
        if last:
            source, parts = results
        else:
            source, *outs, rows = results
    parts = lax.all_to_all(parts, "cls", 0, 0)
    out = pl.pallas_call(
        last_kernel,
        out_shape=own_shape,
        in_specs=[VMEM, VMEM],
        out_specs=HBM,
        scratch_shapes=[pltpu.VMEM((8, SIDE, SIDE), F32), pltpu.SemaphoreType.DMA((8,))],
        compiler_params=PARAMS,
    )(source, parts)
    return out.reshape(8 * SIDE, SIDE)


def solution(mesh):
    split_mesh = Mesh(
        mesh.devices.reshape(mesh.shape["dom"] // 2, 2, mesh.shape["cls"]), ("chip", "core", "cls")
    )
    dom = ("chip", "core")
    return jax.shard_map(
        on_device,
        mesh=split_mesh,
        in_specs=(P(dom, None, None), P(dom), P(dom), P(dom, None, None), P(dom), P(dom, "cls")),
        out_specs=P(dom, "cls"),
        check_vma=False,
    )
```

```python
import functools

import jax
import jax.numpy as jnp
from jax import lax
from jax.experimental import pallas as pl
from jax.experimental.pallas import tpu as pltpu
from jax.sharding import Mesh
from jax.sharding import PartitionSpec as P

CLASSES = 1024
ITERS = 3
SIDE = 128

VMEM = pl.BlockSpec(memory_space=pltpu.VMEM)
SMEM = pl.BlockSpec(memory_space=pltpu.SMEM)
HBM = pl.BlockSpec(memory_space=pltpu.HBM)
F32 = jnp.float32
PARAMS = pltpu.CompilerParams(vmem_limit_bytes=16 * 1024 * 1024)


def shape(*dims):
    return jax.ShapeDtypeStruct(dims, F32)


def shift_right(value, by):
    return lax.shift_right_logical(value, by)


def plan_entries(rows, cols, send):
    core = lax.axis_index("core")
    odd = lax.rem(lax.axis_index("chip"), 2)
    for tile in range(32):
        yield rows[tile]
    for tile in range(32):
        col = cols[tile]
        ghost = jnp.maximum(col - 8, 0)
        offset = shift_right(ghost, 1)
        half = shift_right(offset, 1)
        pair = jnp.where(lax.rem(offset, 2) == 1, 2 * (half ^ odd), 1 + 2 * (half ^ core))
        yield jnp.where(col < 8, col, 8 + 2 * pair + lax.rem(ghost, 2))
    for offset in range(4):
        for within in range(2):
            yield send[0, within, offset]


def row_block(plan, tile):
    return plan[tile]


def operand_block(plan, tile):
    return plan[32 + tile]


def sent_block(plan, offset, within):
    return plan[64 + 2 * offset + within]


def block_at(ref, place):
    return ref[SIDE * place : SIDE * (place + 1), :]


def fill_swaps(source, sums, block_of, outs, rows):
    core = lax.axis_index("core")
    odd = lax.rem(lax.axis_index("chip"), 2)
    rows[0:8, :] = sums
    for out, offset in zip(outs, (3 - 2 * odd, 2 - 2 * core, 1 + 2 * odd, 2 * core)):
        out[2 * SIDE + 2 :, :] = jnp.zeros((6, SIDE), F32)
        for within in range(2):
            block = block_of(offset, within)
            out[SIDE * within : SIDE * (within + 1), :] = source[block]
            out[2 * SIDE + within : 2 * SIDE + within + 1, :] = rows[pl.ds(block, 1), :]


def class_sums(block):
    return jnp.sum(block, axis=0, keepdims=True)


def copy_all(pairs, sems):
    copies = []
    for number, (here, there) in enumerate(pairs):
        copy = pltpu.make_async_copy(here, there, sems.at[number])
        copy.start()
        copies.append(copy)
    return copies


def first_kernel(labels, send, rows, cols, mask, kept, plan, mask_kept, *refs):
    *outs, sums_out, fetched, send_here, rows_here, cols_here, plan_here, sems = refs
    pairs = [(send, send_here), (rows, rows_here), (cols, cols_here)]
    pairs += [(labels.at[block], fetched.at[block]) for block in range(8)]
    copies = copy_all(pairs + [(mask, mask_kept)], sems)
    sums = []
    for block in range(8):
        copies[3 + block].wait()
        value = jnp.transpose(fetched[block])
        kept[block] = value
        sums.append(class_sums(value))
    for copy in copies[:3]:
        copy.wait()
    for place, entry in enumerate(plan_entries(rows_here, cols_here, send_here)):
        plan_here[place] = entry
    plan_copy = pltpu.make_async_copy(plan_here, plan, sems.at[12])
    plan_copy.start()
    block_of = lambda offset, within: send_here[0, within, offset]
    fill_swaps(kept, jnp.concatenate(sums, axis=0), block_of, outs, sums_out)
    copies[11].wait()
    plan_copy.wait()


def mass_kernel(sums, in0, in1, in2, in3, parts):
    received = [ref[2 * SIDE : 2 * SIDE + 2, :] for ref in (in0, in1, in2, in3)]
    partial = jnp.concatenate([sums[...]] + received, axis=0)
    for share in range(8):
        parts[share] = partial


def total_of(parts):
    total = parts[0]
    for share in range(1, 8):
        total = total + parts[share]
    return total


def split(value):
    high = value.astype(jnp.bfloat16)
    low = (value - high.astype(F32)).astype(jnp.bfloat16)
    return high, low


def spread_kernel(first, last, *refs):
    refs = list(refs)
    tiles, plan, mask, source = refs[:4]
    received = refs[4:8]
    parts = refs[8]
    refs = refs[9:]
    anchor = refs.pop(0) if first else mask
    squared = refs.pop(0)
    if last:
        own_parts, *refs = refs
    else:
        *outs, rows_out = refs[:5]
        refs = refs[5:]
    operand, products, plan_here, plan_sem = refs
    plan_copy = pltpu.make_async_copy(plan, plan_here, plan_sem)
    plan_copy.start()
    scale = CLASSES / total_of(parts)
    if first:
        seeded = 64.0 * mask[...].astype(F32)
    for block in range(16):
        if block < 8:
            value = source[block]
        else:
            value = block_at(received[(block - 8) // 2], block % 2)
        value = value * scale[block : block + 1, :]
        if first and block < 8:
            anchor[block] = seeded[block : block + 1, :] * value + 4.0
        high, low = split(value)
        operand[block, :, :SIDE] = high
        operand[block, :, SIDE:] = low
    plan_copy.wait()
    plan = plan_here
    for tile in range(32):
        weights = tiles[tile]
        products[tile] = lax.dot_general(
            operand[operand_block(plan, tile)],
            jnp.concatenate([weights, weights], axis=1),
            (((1,), (1,)), ((), ())),
            preferred_element_type=F32,
        )
    squared[...] = anchor[...]
    for tile in range(32):
        row = row_block(plan, tile)
        squared[row] = squared[row] + products[tile]
    sums = []
    for block in range(8):
        value = squared[block]
        value = value * value
        squared[block] = value
        sums.append(class_sums(value))
    sums = jnp.concatenate(sums, axis=0)
    if last:
        for share in range(8):
            own_parts[share] = sums
    else:
        block_of = functools.partial(sent_block, plan)
        fill_swaps(squared, sums, block_of, outs, rows_out)


def last_kernel(squared, parts, out, scaled, sems):
    scale = CLASSES / total_of(parts)
    copies = []
    for block in range(8):
        scaled[block] = jnp.transpose(squared[block] * scale[block : block + 1, :])
        copy = pltpu.make_async_copy(scaled.at[block], out.at[block], sems.at[block])
        copy.start()
        copies.append(copy)
    for copy in copies:
        copy.wait()


def on_device(tiles, tile_rows, tile_cols, send_lists, seed_mask, labels):
    dom = ("chip", "core")
    count = 2 * lax.axis_size("chip")
    swaps = [
        [(i, (i + (2 if i // 2 % 2 else -2)) % count) for i in range(count)],
        [(i, (i + (1 if i % 2 else -1)) % count) for i in range(count)],
        [(i, (i + (-2 if i // 2 % 2 else 2)) % count) for i in range(count)],
        [(i, i ^ 1) for i in range(count)],
    ]
    send_lists = jnp.transpose(send_lists, (0, 2, 1))
    own_shape = shape(8, SIDE, SIDE)
    sent_shapes = [shape(2 * SIDE + 8, SIDE)] * 4 + [shape(8, SIDE)]
    blocks, tile_rows, tile_cols, send_lists, mask = [
        pltpu.with_memory_space_constraint(value, pltpu.HBM)
        for value in (
            labels.reshape(8, SIDE, SIDE),
            tile_rows,
            tile_cols,
            send_lists,
            seed_mask.reshape(8, SIDE),
        )
    ]
    plan_shape = jax.ShapeDtypeStruct((72,), jnp.int32)
    source, plan, mask, *outs, rows = pl.pallas_call(
        first_kernel,
        out_shape=[own_shape, plan_shape, jax.ShapeDtypeStruct((8, SIDE), jnp.int32)] + sent_shapes,
        in_specs=[HBM] * 5,
        out_specs=[VMEM] * 8,
        scratch_shapes=[
            pltpu.VMEM((8, SIDE, SIDE), F32),
            pltpu.SMEM((1, 2, 4), jnp.int32),
            pltpu.SMEM((32,), jnp.int32),
            pltpu.SMEM((32,), jnp.int32),
            pltpu.SMEM((72,), jnp.int32),
            pltpu.SemaphoreType.DMA((13,)),
        ],
        compiler_params=PARAMS,
        cost_estimate=pl.CostEstimate(flops=1 << 20, bytes_accessed=1 << 20, transcendentals=0),
    )(blocks, send_lists, tile_rows, tile_cols, mask)
    anchor = None
    for iteration in range(ITERS):
        first = iteration == 0
        last = iteration == ITERS - 1
        received = [lax.ppermute(out, dom, swap) for out, swap in zip(outs, swaps)]
        parts = pl.pallas_call(
            mass_kernel,
            out_shape=shape(8, 16, SIDE),
            in_specs=[VMEM] * 5,
            out_specs=VMEM,
            compiler_params=PARAMS,
        )(rows, *received)
        parts = lax.all_to_all(parts, "cls", 0, 0)
        out_shape = [own_shape] * (2 if first else 1)
        out_shape += [shape(8, 8, SIDE)] if last else sent_shapes
        results = pl.pallas_call(
            lambda *refs, first=first, last=last: spread_kernel(first, last, *refs),
            out_shape=out_shape,
            in_specs=[VMEM] * 9,
            out_specs=[VMEM] * len(out_shape),
            scratch_shapes=[
                pltpu.VMEM((16, SIDE, 2 * SIDE), jnp.bfloat16),
                pltpu.VMEM((32, SIDE, SIDE), F32),
                pltpu.SMEM((72,), jnp.int32),
                pltpu.SemaphoreType.DMA,
            ],
            compiler_params=PARAMS,
        )(tiles, plan, mask if first else anchor, source, *received, parts)
        if first:
            anchor, *results = results
        if last:
            source, parts = results
        else:
            source, *outs, rows = results
    parts = lax.all_to_all(parts, "cls", 0, 0)
    out = pl.pallas_call(
        last_kernel,
        out_shape=own_shape,
        in_specs=[VMEM, VMEM],
        out_specs=HBM,
        scratch_shapes=[pltpu.VMEM((8, SIDE, SIDE), F32), pltpu.SemaphoreType.DMA((8,))],
        compiler_params=PARAMS,
    )(source, parts)
    return out.reshape(8 * SIDE, SIDE)


def solution(mesh):
    split_mesh = Mesh(
        mesh.devices.reshape(mesh.shape["dom"] // 2, 2, mesh.shape["cls"]), ("chip", "core", "cls")
    )
    dom = ("chip", "core")
    return jax.shard_map(
        on_device,
        mesh=split_mesh,
        in_specs=(P(dom, None, None), P(dom), P(dom), P(dom, None, None), P(dom), P(dom, "cls")),
        out_specs=P(dom, "cls"),
        check_vma=False,
    )
```

```python
import functools

import jax
import jax.numpy as jnp
from jax import lax
from jax.experimental import pallas as pl
from jax.experimental.pallas import tpu as pltpu
from jax.sharding import Mesh
from jax.sharding import PartitionSpec as P

CLASSES = 1024
ITERS = 3
SIDE = 128

VMEM = pl.BlockSpec(memory_space=pltpu.VMEM)
SMEM = pl.BlockSpec(memory_space=pltpu.SMEM)
HBM = pl.BlockSpec(memory_space=pltpu.HBM)
F32 = jnp.float32
PARAMS = pltpu.CompilerParams(vmem_limit_bytes=16 * 1024 * 1024)


def shape(*dims):
    return jax.ShapeDtypeStruct(dims, F32)


def shift_right(value, by):
    return lax.shift_right_logical(value, by)


def plan_entries(rows, cols, send):
    core = lax.axis_index("core")
    for tile in range(32):
        yield rows[tile]
    for tile in range(32):
        col = cols[tile]
        ghost = jnp.maximum(col - 8, 0)
        offset = shift_right(ghost, 1)
        half = shift_right(offset, 1)
        pair = jnp.where(lax.rem(offset, 2) == 1, 2 * half, 1 + 2 * (half ^ core))
        yield jnp.where(col < 8, col, 8 + 2 * pair + lax.rem(ghost, 2))
    for offset in range(4):
        for within in range(2):
            yield send[0, within, offset]


def row_block(plan, tile):
    return plan[tile]


def operand_block(plan, tile):
    return plan[32 + tile]


def sent_block(plan, offset, within):
    return plan[64 + 2 * offset + within]


def block_at(ref, place):
    return ref[SIDE * place : SIDE * (place + 1), :]


def fill_swaps(source, sums, block_of, outs, rows):
    core = lax.axis_index("core")
    rows[0:8, :] = sums
    for out, offset in zip(outs, (1, 2 - 2 * core, 3, 2 * core)):
        out[2 * SIDE + 2 :, :] = jnp.zeros((6, SIDE), F32)
        for within in range(2):
            block = block_of(offset, within)
            out[SIDE * within : SIDE * (within + 1), :] = source[block]
            out[2 * SIDE + within : 2 * SIDE + within + 1, :] = rows[pl.ds(block, 1), :]


def class_sums(block):
    return jnp.sum(block, axis=0, keepdims=True)


def copy_all(pairs, sems):
    copies = []
    for number, (here, there) in enumerate(pairs):
        copy = pltpu.make_async_copy(here, there, sems.at[number])
        copy.start()
        copies.append(copy)
    return copies


def first_kernel(labels, send, rows, cols, mask, kept, plan, mask_kept, *refs):
    *outs, sums_out, fetched, send_here, rows_here, cols_here, plan_here, sems = refs
    pairs = [(send, send_here), (rows, rows_here), (cols, cols_here)]
    pairs += [(labels.at[block], fetched.at[block]) for block in range(8)]
    copies = copy_all(pairs + [(mask, mask_kept)], sems)
    for copy in copies[:3]:
        copy.wait()
    for place, entry in enumerate(plan_entries(rows_here, cols_here, send_here)):
        plan_here[place] = entry
    plan_copy = pltpu.make_async_copy(plan_here, plan, sems.at[12])
    plan_copy.start()
    sums = []
    for block in range(8):
        copies[3 + block].wait()
        value = jnp.transpose(fetched[block])
        kept[block] = value
        sums.append(class_sums(value))
    block_of = lambda offset, within: send_here[0, within, offset]
    fill_swaps(kept, jnp.concatenate(sums, axis=0), block_of, outs, sums_out)
    copies[11].wait()
    plan_copy.wait()


def mass_kernel(sums, in0, in1, in2, in3, parts):
    received = [ref[2 * SIDE : 2 * SIDE + 2, :] for ref in (in0, in1, in2, in3)]
    partial = jnp.concatenate([sums[...]] + received, axis=0)
    for share in range(8):
        parts[share] = partial


def total_of(parts):
    total = parts[0]
    for share in range(1, 8):
        total = total + parts[share]
    return total


def split(value):
    high = value.astype(jnp.bfloat16)
    low = (value - high.astype(F32)).astype(jnp.bfloat16)
    return high, low


def spread_kernel(first, last, *refs):
    refs = list(refs)
    tiles, plan, mask, source = refs[:4]
    received = refs[4:8]
    parts = refs[8]
    refs = refs[9:]
    anchor = refs.pop(0) if first else mask
    squared = refs.pop(0)
    if last:
        own_parts, *refs = refs
    else:
        *outs, rows_out = refs[:5]
        refs = refs[5:]
    operand, products, plan_here, plan_sem = refs
    plan_copy = pltpu.make_async_copy(plan, plan_here, plan_sem)
    plan_copy.start()
    scale = CLASSES / total_of(parts)
    if first:
        seeded = 64.0 * mask[...].astype(F32)
    for block in range(16):
        if block < 8:
            value = source[block]
        else:
            value = block_at(received[(block - 8) // 2], block % 2)
        value = value * scale[block : block + 1, :]
        if first and block < 8:
            anchor[block] = seeded[block : block + 1, :] * value + 4.0
        high, low = split(value)
        operand[block, :SIDE, :] = high
        operand[block, SIDE:, :] = low
    plan_copy.wait()
    plan = plan_here
    for tile in range(32):
        halves = lax.dot_general(
            operand[operand_block(plan, tile)],
            tiles[tile],
            (((1,), (1,)), ((), ())),
            preferred_element_type=F32,
        )
        products[tile] = halves[:SIDE] + halves[SIDE:]
    squared[...] = anchor[...]
    for tile in range(32):
        row = row_block(plan, tile)
        squared[row] = squared[row] + products[tile]
    sums = []
    for block in range(8):
        value = squared[block]
        value = value * value
        squared[block] = value
        sums.append(class_sums(value))
    sums = jnp.concatenate(sums, axis=0)
    if last:
        for share in range(8):
            own_parts[share] = sums
    else:
        block_of = functools.partial(sent_block, plan)
        fill_swaps(squared, sums, block_of, outs, rows_out)


def last_kernel(squared, parts, out, scaled, sems):
    scale = CLASSES / total_of(parts)
    copies = []
    for block in range(8):
        scaled[block] = jnp.transpose(squared[block] * scale[block : block + 1, :])
        copy = pltpu.make_async_copy(scaled.at[block], out.at[block], sems.at[block])
        copy.start()
        copies.append(copy)
    for copy in copies:
        copy.wait()


def on_device(tiles, tile_rows, tile_cols, send_lists, seed_mask, labels):
    dom = ("chip", "core")
    count = 2 * lax.axis_size("chip")
    swaps = [
        [(i, (i + 2) % count) for i in range(count)],
        [(i, (i + (1 if i % 2 else -1)) % count) for i in range(count)],
        [(i, (i - 2) % count) for i in range(count)],
        [(i, i ^ 1) for i in range(count)],
    ]
    send_lists = jnp.transpose(send_lists, (0, 2, 1))
    own_shape = shape(8, SIDE, SIDE)
    sent_shapes = [shape(2 * SIDE + 8, SIDE)] * 4 + [shape(8, SIDE)]
    blocks, tile_rows, tile_cols, send_lists, mask = [
        pltpu.with_memory_space_constraint(value, pltpu.HBM)
        for value in (
            labels.reshape(8, SIDE, SIDE),
            tile_rows,
            tile_cols,
            send_lists,
            seed_mask.reshape(8, SIDE),
        )
    ]
    plan_shape = jax.ShapeDtypeStruct((72,), jnp.int32)
    source, plan, mask, *outs, rows = pl.pallas_call(
        first_kernel,
        out_shape=[own_shape, plan_shape, jax.ShapeDtypeStruct((8, SIDE), jnp.int32)] + sent_shapes,
        in_specs=[HBM] * 5,
        out_specs=[VMEM] * 8,
        scratch_shapes=[
            pltpu.VMEM((8, SIDE, SIDE), F32),
            pltpu.SMEM((1, 2, 4), jnp.int32),
            pltpu.SMEM((32,), jnp.int32),
            pltpu.SMEM((32,), jnp.int32),
            pltpu.SMEM((72,), jnp.int32),
            pltpu.SemaphoreType.DMA((13,)),
        ],
        compiler_params=PARAMS,
        cost_estimate=pl.CostEstimate(flops=1 << 20, bytes_accessed=1 << 20, transcendentals=0),
    )(blocks, send_lists, tile_rows, tile_cols, mask)
    anchor = None
    for iteration in range(ITERS):
        first = iteration == 0
        last = iteration == ITERS - 1
        received = [lax.ppermute(out, dom, swap) for out, swap in zip(outs, swaps)]
        parts = pl.pallas_call(
            mass_kernel,
            out_shape=shape(8, 16, SIDE),
            in_specs=[VMEM] * 5,
            out_specs=VMEM,
            compiler_params=PARAMS,
        )(rows, *received)
        parts = lax.all_to_all(parts, "cls", 0, 0)
        out_shape = [own_shape] * (2 if first else 1)
        out_shape += [shape(8, 8, SIDE)] if last else sent_shapes
        results = pl.pallas_call(
            lambda *refs, first=first, last=last: spread_kernel(first, last, *refs),
            out_shape=out_shape,
            in_specs=[VMEM] * 9,
            out_specs=[VMEM] * len(out_shape),
            scratch_shapes=[
                pltpu.VMEM((16, 2 * SIDE, SIDE), jnp.bfloat16),
                pltpu.VMEM((32, SIDE, SIDE), F32),
                pltpu.SMEM((72,), jnp.int32),
                pltpu.SemaphoreType.DMA,
            ],
            compiler_params=PARAMS,
        )(tiles, plan, mask if first else anchor, source, *received, parts)
        if first:
            anchor, *results = results
        if last:
            source, parts = results
        else:
            source, *outs, rows = results
    parts = lax.all_to_all(parts, "cls", 0, 0)
    out = pl.pallas_call(
        last_kernel,
        out_shape=own_shape,
        in_specs=[VMEM, VMEM],
        out_specs=HBM,
        scratch_shapes=[pltpu.VMEM((8, SIDE, SIDE), F32), pltpu.SemaphoreType.DMA((8,))],
        compiler_params=PARAMS,
    )(source, parts)
    return out.reshape(8 * SIDE, SIDE)


def solution(mesh):
    split_mesh = Mesh(
        mesh.devices.reshape(mesh.shape["dom"] // 2, 2, mesh.shape["cls"]), ("chip", "core", "cls")
    )
    dom = ("chip", "core")
    return jax.shard_map(
        on_device,
        mesh=split_mesh,
        in_specs=(P(dom, None, None), P(dom), P(dom), P(dom, None, None), P(dom), P(dom, "cls")),
        out_specs=P(dom, "cls"),
        check_vma=False,
    )
```

```python
import functools

import jax
import jax.numpy as jnp
from jax import lax
from jax.experimental import pallas as pl
from jax.experimental.pallas import tpu as pltpu
from jax.sharding import Mesh
from jax.sharding import PartitionSpec as P

CLASSES = 1024
ITERS = 3
SIDE = 128

VMEM = pl.BlockSpec(memory_space=pltpu.VMEM)
SMEM = pl.BlockSpec(memory_space=pltpu.SMEM)
HBM = pl.BlockSpec(memory_space=pltpu.HBM)
F32 = jnp.float32
PARAMS = pltpu.CompilerParams(vmem_limit_bytes=16 * 1024 * 1024)


def shape(*dims):
    return jax.ShapeDtypeStruct(dims, F32)


def shift_right(value, by):
    return lax.shift_right_logical(value, by)


def plan_entries(rows, cols, send):
    core = lax.axis_index("core")
    for tile in range(32):
        yield rows[tile]
    for tile in range(32):
        col = cols[tile]
        ghost = jnp.maximum(col - 8, 0)
        offset = shift_right(ghost, 1)
        half = shift_right(offset, 1)
        pair = jnp.where(lax.rem(offset, 2) == 1, 2 * (half ^ core), 1 + 2 * (half ^ core))
        yield jnp.where(col < 8, col, 8 + 2 * pair + lax.rem(ghost, 2))
    for offset in range(4):
        for within in range(2):
            yield send[0, within, offset]


def row_block(plan, tile):
    return plan[tile]


def operand_block(plan, tile):
    return plan[32 + tile]


def sent_block(plan, offset, within):
    return plan[64 + 2 * offset + within]


def block_at(ref, place):
    return ref[SIDE * place : SIDE * (place + 1), :]


def fill_swaps(source, sums, block_of, outs, rows):
    core = lax.axis_index("core")
    rows[0:8, :] = sums
    for out, offset in zip(outs, (1 + 2 * core, 2 - 2 * core, 3 - 2 * core, 2 * core)):
        out[2 * SIDE + 2 :, :] = jnp.zeros((6, SIDE), F32)
        for within in range(2):
            block = block_of(offset, within)
            out[SIDE * within : SIDE * (within + 1), :] = source[block]
            out[2 * SIDE + within : 2 * SIDE + within + 1, :] = rows[pl.ds(block, 1), :]


def class_sums(block):
    return jnp.sum(block, axis=0, keepdims=True)


def copy_all(pairs, sems):
    copies = []
    for number, (here, there) in enumerate(pairs):
        copy = pltpu.make_async_copy(here, there, sems.at[number])
        copy.start()
        copies.append(copy)
    return copies


def first_kernel(labels, send, rows, cols, mask, kept, plan, mask_kept, *refs):
    *outs, sums_out, fetched, send_here, rows_here, cols_here, plan_here, sems = refs
    pairs = [(send, send_here), (rows, rows_here), (cols, cols_here)]
    pairs += [(labels.at[block], fetched.at[block]) for block in range(8)]
    copies = copy_all(pairs + [(mask, mask_kept)], sems)
    for copy in copies[:3]:
        copy.wait()
    for place, entry in enumerate(plan_entries(rows_here, cols_here, send_here)):
        plan_here[place] = entry
    plan_copy = pltpu.make_async_copy(plan_here, plan, sems.at[12])
    plan_copy.start()
    sums = []
    for block in range(8):
        copies[3 + block].wait()
        value = jnp.transpose(fetched[block])
        kept[block] = value
        sums.append(class_sums(value))
    block_of = lambda offset, within: send_here[0, within, offset]
    fill_swaps(kept, jnp.concatenate(sums, axis=0), block_of, outs, sums_out)
    copies[11].wait()
    plan_copy.wait()


def mass_kernel(sums, in0, in1, in2, in3, parts):
    received = [ref[2 * SIDE : 2 * SIDE + 2, :] for ref in (in0, in1, in2, in3)]
    partial = jnp.concatenate([sums[...]] + received, axis=0)
    for share in range(8):
        parts[share] = partial


def total_of(parts):
    total = parts[0]
    for share in range(1, 8):
        total = total + parts[share]
    return total


def split(value):
    high = value.astype(jnp.bfloat16)
    low = (value - high.astype(F32)).astype(jnp.bfloat16)
    return high, low


def spread_kernel(first, last, *refs):
    refs = list(refs)
    tiles, plan, mask, source = refs[:4]
    received = refs[4:8]
    parts = refs[8]
    refs = refs[9:]
    anchor = refs.pop(0) if first else mask
    squared = refs.pop(0)
    if last:
        own_parts, *refs = refs
    else:
        *outs, rows_out = refs[:5]
        refs = refs[5:]
    operand, products, plan_here, plan_sem = refs
    plan_copy = pltpu.make_async_copy(plan, plan_here, plan_sem)
    plan_copy.start()
    scale = CLASSES / total_of(parts)
    if first:
        seeded = 64.0 * mask[...].astype(F32)
    for block in range(16):
        if block < 8:
            value = source[block]
        else:
            value = block_at(received[(block - 8) // 2], block % 2)
        value = value * scale[block : block + 1, :]
        if first and block < 8:
            anchor[block] = seeded[block : block + 1, :] * value + 4.0
        high, low = split(value)
        operand[block, :SIDE, :] = high
        operand[block, SIDE:, :] = low
    plan_copy.wait()
    plan = plan_here
    for tile in range(32):
        halves = lax.dot_general(
            operand[operand_block(plan, tile)],
            tiles[tile],
            (((1,), (1,)), ((), ())),
            preferred_element_type=F32,
        )
        products[tile] = halves[:SIDE] + halves[SIDE:]
    squared[...] = anchor[...]
    for tile in range(32):
        row = row_block(plan, tile)
        squared[row] = squared[row] + products[tile]
    sums = []
    for block in range(8):
        value = squared[block]
        value = value * value
        squared[block] = value
        sums.append(class_sums(value))
    sums = jnp.concatenate(sums, axis=0)
    if last:
        for share in range(8):
            own_parts[share] = sums
    else:
        block_of = functools.partial(sent_block, plan)
        fill_swaps(squared, sums, block_of, outs, rows_out)


def last_kernel(squared, parts, out, scaled, sems):
    scale = CLASSES / total_of(parts)
    copies = []
    for block in range(8):
        scaled[block] = jnp.transpose(squared[block] * scale[block : block + 1, :])
        copy = pltpu.make_async_copy(scaled.at[block], out.at[block], sems.at[block])
        copy.start()
        copies.append(copy)
    for copy in copies:
        copy.wait()


def on_device(tiles, tile_rows, tile_cols, send_lists, seed_mask, labels):
    dom = ("chip", "core")
    count = 2 * lax.axis_size("chip")
    swaps = [
        [(i, (i + (-2 if i % 2 else 2)) % count) for i in range(count)],
        [(i, (i + (1 if i % 2 else -1)) % count) for i in range(count)],
        [(i, (i + (2 if i % 2 else -2)) % count) for i in range(count)],
        [(i, i ^ 1) for i in range(count)],
    ]
    send_lists = jnp.transpose(send_lists, (0, 2, 1))
    own_shape = shape(8, SIDE, SIDE)
    sent_shapes = [shape(2 * SIDE + 8, SIDE)] * 4 + [shape(8, SIDE)]
    blocks, tile_rows, tile_cols, send_lists, mask = [
        pltpu.with_memory_space_constraint(value, pltpu.HBM)
        for value in (
            labels.reshape(8, SIDE, SIDE),
            tile_rows,
            tile_cols,
            send_lists,
            seed_mask.reshape(8, SIDE),
        )
    ]
    plan_shape = jax.ShapeDtypeStruct((72,), jnp.int32)
    source, plan, mask, *outs, rows = pl.pallas_call(
        first_kernel,
        out_shape=[own_shape, plan_shape, jax.ShapeDtypeStruct((8, SIDE), jnp.int32)] + sent_shapes,
        in_specs=[HBM] * 5,
        out_specs=[VMEM] * 8,
        scratch_shapes=[
            pltpu.VMEM((8, SIDE, SIDE), F32),
            pltpu.SMEM((1, 2, 4), jnp.int32),
            pltpu.SMEM((32,), jnp.int32),
            pltpu.SMEM((32,), jnp.int32),
            pltpu.SMEM((72,), jnp.int32),
            pltpu.SemaphoreType.DMA((13,)),
        ],
        compiler_params=PARAMS,
        cost_estimate=pl.CostEstimate(flops=1 << 20, bytes_accessed=1 << 20, transcendentals=0),
    )(blocks, send_lists, tile_rows, tile_cols, mask)
    anchor = None
    for iteration in range(ITERS):
        first = iteration == 0
        last = iteration == ITERS - 1
        received = [lax.ppermute(out, dom, swap) for out, swap in zip(outs, swaps)]
        parts = pl.pallas_call(
            mass_kernel,
            out_shape=shape(8, 16, SIDE),
            in_specs=[VMEM] * 5,
            out_specs=VMEM,
            compiler_params=PARAMS,
        )(rows, *received)
        parts = lax.all_to_all(parts, "cls", 0, 0)
        out_shape = [own_shape] * (2 if first else 1)
        out_shape += [shape(8, 8, SIDE)] if last else sent_shapes
        results = pl.pallas_call(
            lambda *refs, first=first, last=last: spread_kernel(first, last, *refs),
            out_shape=out_shape,
            in_specs=[VMEM] * 9,
            out_specs=[VMEM] * len(out_shape),
            scratch_shapes=[
                pltpu.VMEM((16, 2 * SIDE, SIDE), jnp.bfloat16),
                pltpu.VMEM((32, SIDE, SIDE), F32),
                pltpu.SMEM((72,), jnp.int32),
                pltpu.SemaphoreType.DMA,
            ],
            compiler_params=PARAMS,
        )(tiles, plan, mask if first else anchor, source, *received, parts)
        if first:
            anchor, *results = results
        if last:
            source, parts = results
        else:
            source, *outs, rows = results
    parts = lax.all_to_all(parts, "cls", 0, 0)
    out = pl.pallas_call(
        last_kernel,
        out_shape=own_shape,
        in_specs=[VMEM, VMEM],
        out_specs=HBM,
        scratch_shapes=[pltpu.VMEM((8, SIDE, SIDE), F32), pltpu.SemaphoreType.DMA((8,))],
        compiler_params=PARAMS,
    )(source, parts)
    return out.reshape(8 * SIDE, SIDE)


def solution(mesh):
    split_mesh = Mesh(
        mesh.devices.reshape(mesh.shape["dom"] // 2, 2, mesh.shape["cls"]), ("chip", "core", "cls")
    )
    dom = ("chip", "core")
    return jax.shard_map(
        on_device,
        mesh=split_mesh,
        in_specs=(P(dom, None, None), P(dom), P(dom), P(dom, None, None), P(dom), P(dom, "cls")),
        out_specs=P(dom, "cls"),
        check_vma=False,
    )
```

```python
import functools

import jax
import jax.numpy as jnp
from jax import lax
from jax.experimental import pallas as pl
from jax.experimental.pallas import tpu as pltpu
from jax.sharding import Mesh
from jax.sharding import PartitionSpec as P

CLASSES = 1024
ITERS = 3
SIDE = 128

VMEM = pl.BlockSpec(memory_space=pltpu.VMEM)
SMEM = pl.BlockSpec(memory_space=pltpu.SMEM)
HBM = pl.BlockSpec(memory_space=pltpu.HBM)
F32 = jnp.float32
PARAMS = pltpu.CompilerParams(vmem_limit_bytes=16 * 1024 * 1024)


def shape(*dims):
    return jax.ShapeDtypeStruct(dims, F32)


def shift_right(value, by):
    return lax.shift_right_logical(value, by)


def plan_entries(cols, send):
    core = lax.axis_index("core")
    for tile in range(32):
        col = cols[tile]
        ghost = jnp.maximum(col - 8, 0)
        offset = shift_right(ghost, 1)
        half = shift_right(offset, 1)
        pair = jnp.where(lax.rem(offset, 2) == 1, 2 * (half ^ core), 1 + 2 * (half ^ core))
        yield jnp.where(col < 8, col, 8 + 2 * pair + lax.rem(ghost, 2))
    for offset in range(4):
        for within in range(2):
            yield send[0, within, offset]


def operand_block(plan, tile):
    return plan[tile]


def sent_block(plan, offset, within):
    return plan[32 + 2 * offset + within]


def block_at(ref, place):
    return ref[SIDE * place : SIDE * (place + 1), :]


def fill_swaps(source, sums, block_of, outs, rows):
    core = lax.axis_index("core")
    rows[0:8, :] = sums
    for out, offset in zip(outs, (1 + 2 * core, 2 - 2 * core, 3 - 2 * core, 2 * core)):
        out[2 * SIDE + 2 :, :] = jnp.zeros((6, SIDE), F32)
        for within in range(2):
            block = block_of(offset, within)
            out[SIDE * within : SIDE * (within + 1), :] = source[block]
            out[2 * SIDE + within : 2 * SIDE + within + 1, :] = rows[pl.ds(block, 1), :]


def class_sums(block):
    return jnp.sum(block, axis=0, keepdims=True)


def copy_all(pairs, sems):
    copies = []
    for number, (here, there) in enumerate(pairs):
        copy = pltpu.make_async_copy(here, there, sems.at[number])
        copy.start()
        copies.append(copy)
    return copies


def first_kernel(labels, send, rows, cols, mask, kept, plan, rows_kept, mask_kept, *refs):
    *outs, sums_out, fetched, send_here, cols_here, plan_here, sems = refs
    pairs = [(send, send_here), (cols, cols_here)]
    pairs += [(labels.at[block], fetched.at[block]) for block in range(8)]
    copies = copy_all(pairs + [(mask, mask_kept), (rows, rows_kept)], sems)
    for copy in copies[:2]:
        copy.wait()
    for place, entry in enumerate(plan_entries(cols_here, send_here)):
        plan_here[place] = entry
    plan_copy = pltpu.make_async_copy(plan_here, plan, sems.at[12])
    plan_copy.start()
    sums = []
    for block in range(8):
        copies[2 + block].wait()
        value = jnp.transpose(fetched[block])
        kept[block] = value
        sums.append(class_sums(value))
    block_of = lambda offset, within: send_here[0, within, offset]
    fill_swaps(kept, jnp.concatenate(sums, axis=0), block_of, outs, sums_out)
    copies[10].wait()
    copies[11].wait()
    plan_copy.wait()


def mass_kernel(sums, in0, in1, in2, in3, parts):
    received = [ref[2 * SIDE : 2 * SIDE + 2, :] for ref in (in0, in1, in2, in3)]
    partial = jnp.concatenate([sums[...]] + received, axis=0)
    for share in range(8):
        parts[share] = partial


def total_of(parts):
    total = parts[0]
    for share in range(1, 8):
        total = total + parts[share]
    return total


def split(value):
    high = value.astype(jnp.bfloat16)
    low = (value - high.astype(F32)).astype(jnp.bfloat16)
    return high, low


def spread_kernel(first, last, *refs):
    refs = list(refs)
    tiles, plan, rows, mask, source = refs[:5]
    received = refs[5:9]
    parts = refs[9]
    refs = refs[10:]
    anchor = refs.pop(0) if first else mask
    squared = refs.pop(0)
    if last:
        own_parts, *refs = refs
    else:
        *outs, rows_out = refs[:5]
        refs = refs[5:]
    operand, products, plan_here, rows_here, sems = refs
    copies = copy_all([(plan, plan_here), (rows, rows_here)], sems)
    scale = CLASSES / total_of(parts)
    if first:
        seeded = 64.0 * mask[...].astype(F32)
    for block in range(16):
        if block < 8:
            value = source[block]
        else:
            value = block_at(received[(block - 8) // 2], block % 2)
        value = value * scale[block : block + 1, :]
        if first and block < 8:
            anchor[block] = seeded[block : block + 1, :] * value + 4.0
        high, low = split(value)
        operand[block, :SIDE, :] = high
        operand[block, SIDE:, :] = low
    for copy in copies:
        copy.wait()
    plan = plan_here
    for tile in range(32):
        halves = lax.dot_general(
            operand[operand_block(plan, tile)],
            tiles[tile],
            (((1,), (1,)), ((), ())),
            preferred_element_type=F32,
        )
        products[tile] = halves[:SIDE] + halves[SIDE:]
    squared[...] = anchor[...]
    for tile in range(32):
        row = rows_here[tile]
        squared[row] = squared[row] + products[tile]
    sums = []
    for block in range(8):
        value = squared[block]
        value = value * value
        squared[block] = value
        sums.append(class_sums(value))
    sums = jnp.concatenate(sums, axis=0)
    if last:
        for share in range(8):
            own_parts[share] = sums
    else:
        block_of = functools.partial(sent_block, plan)
        fill_swaps(squared, sums, block_of, outs, rows_out)


def last_kernel(squared, parts, out, scaled, sems):
    scale = CLASSES / total_of(parts)
    copies = []
    for block in range(8):
        scaled[block] = jnp.transpose(squared[block] * scale[block : block + 1, :])
        copy = pltpu.make_async_copy(scaled.at[block], out.at[block], sems.at[block])
        copy.start()
        copies.append(copy)
    for copy in copies:
        copy.wait()


def on_device(tiles, tile_rows, tile_cols, send_lists, seed_mask, labels):
    dom = ("chip", "core")
    count = 2 * lax.axis_size("chip")
    swaps = [
        [(i, (i + (-2 if i % 2 else 2)) % count) for i in range(count)],
        [(i, (i + (1 if i % 2 else -1)) % count) for i in range(count)],
        [(i, (i + (2 if i % 2 else -2)) % count) for i in range(count)],
        [(i, i ^ 1) for i in range(count)],
    ]
    send_lists = jnp.transpose(send_lists, (0, 2, 1))
    own_shape = shape(8, SIDE, SIDE)
    sent_shapes = [shape(2 * SIDE + 8, SIDE)] * 4 + [shape(8, SIDE)]
    blocks, tile_rows, tile_cols, send_lists, mask = [
        pltpu.with_memory_space_constraint(value, pltpu.HBM)
        for value in (
            labels.reshape(8, SIDE, SIDE),
            tile_rows,
            tile_cols,
            send_lists,
            seed_mask.reshape(8, SIDE),
        )
    ]
    plan_shape = jax.ShapeDtypeStruct((40,), jnp.int32)
    tile_shape = jax.ShapeDtypeStruct((32,), jnp.int32)
    source, plan, tile_rows, mask, *outs, rows = pl.pallas_call(
        first_kernel,
        out_shape=[own_shape, plan_shape, tile_shape, jax.ShapeDtypeStruct((8, SIDE), jnp.int32)] + sent_shapes,
        in_specs=[HBM] * 5,
        out_specs=[VMEM] * 9,
        scratch_shapes=[
            pltpu.VMEM((8, SIDE, SIDE), F32),
            pltpu.SMEM((1, 2, 4), jnp.int32),
            pltpu.SMEM((32,), jnp.int32),
            pltpu.SMEM((40,), jnp.int32),
            pltpu.SemaphoreType.DMA((13,)),
        ],
        compiler_params=PARAMS,
        cost_estimate=pl.CostEstimate(flops=1 << 20, bytes_accessed=1 << 20, transcendentals=0),
    )(blocks, send_lists, tile_rows, tile_cols, mask)
    anchor = None
    for iteration in range(ITERS):
        first = iteration == 0
        last = iteration == ITERS - 1
        received = [lax.ppermute(out, dom, swap) for out, swap in zip(outs, swaps)]
        parts = pl.pallas_call(
            mass_kernel,
            out_shape=shape(8, 16, SIDE),
            in_specs=[VMEM] * 5,
            out_specs=VMEM,
            compiler_params=PARAMS,
        )(rows, *received)
        parts = lax.all_to_all(parts, "cls", 0, 0)
        out_shape = [own_shape] * (2 if first else 1)
        out_shape += [shape(8, 8, SIDE)] if last else sent_shapes
        results = pl.pallas_call(
            lambda *refs, first=first, last=last: spread_kernel(first, last, *refs),
            out_shape=out_shape,
            in_specs=[VMEM] * 10,
            out_specs=[VMEM] * len(out_shape),
            scratch_shapes=[
                pltpu.VMEM((16, 2 * SIDE, SIDE), jnp.bfloat16),
                pltpu.VMEM((32, SIDE, SIDE), F32),
                pltpu.SMEM((40,), jnp.int32),
                pltpu.SMEM((32,), jnp.int32),
                pltpu.SemaphoreType.DMA((2,)),
            ],
            compiler_params=PARAMS,
        )(tiles, plan, tile_rows, mask if first else anchor, source, *received, parts)
        if first:
            anchor, *results = results
        if last:
            source, parts = results
        else:
            source, *outs, rows = results
    parts = lax.all_to_all(parts, "cls", 0, 0)
    out = pl.pallas_call(
        last_kernel,
        out_shape=own_shape,
        in_specs=[VMEM, VMEM],
        out_specs=HBM,
        scratch_shapes=[pltpu.VMEM((8, SIDE, SIDE), F32), pltpu.SemaphoreType.DMA((8,))],
        compiler_params=PARAMS,
    )(source, parts)
    return out.reshape(8 * SIDE, SIDE)


def solution(mesh):
    split_mesh = Mesh(
        mesh.devices.reshape(mesh.shape["dom"] // 2, 2, mesh.shape["cls"]), ("chip", "core", "cls")
    )
    dom = ("chip", "core")
    return jax.shard_map(
        on_device,
        mesh=split_mesh,
        in_specs=(P(dom, None, None), P(dom), P(dom), P(dom, None, None), P(dom), P(dom, "cls")),
        out_specs=P(dom, "cls"),
        check_vma=False,
    )
```
